512 devices in a mesh: depth: 32 (over x, y, z_hi), height: 16 (over z_lo, core).
Axes of the slice: x: 4, y: 4, z: 16 (z_hi: 2, z_lo: 8; z = z_hi * 8 + z_lo), core: 2. Of those that a mesh axis runs over, the one named last changes fastest.
Arguments:
- volume: bfloat16 [64, 64, 64, 128], P(None, 'depth', 'height'), may hold values from -6 to 6
- kernel_one: bfloat16 [3, 3, 3, 64, 128], replicated, may hold values from -0.15625 to 0.15625
- kernel_two: bfloat16 [3, 3, 3, 128, 128], replicated, may hold values from -0.109375 to 0.109375
- cotangent: bfloat16 [128, 32, 32, 64], P('height', 'depth'), may hold values from -6 to 6
Outputs:
- next_acts: bfloat16 [128, 32, 32, 64], P('height', 'depth')
- volume_grad: bfloat16 [64, 64, 64, 128], P(None, 'depth', 'height')
- kernel_one_grad: float32 [3, 3, 3, 64, 128], P(None, None, None, 'depth', 'height')
- kernel_two_grad: float32 [3, 3, 3, 128, 128], P(None, None, None, 'depth', 'height')
The draws below stay inside these ranges and needn't reach their ends.
All inputs are finite; a program needn't handle non-finite values.
Results may differ from the reference program's by a relative error of at most 0.0051.
Values may be sent and summed in bfloat16 or wider, within the bound.
No kernel may reach another device: no remote copies, remote signals or barrier semaphores. Data moves between devices by JAX's collectives and lax.ppermute only.
A program may use at most 64 MiB of HBM per device.

```python
import jax
import jax.numpy as jnp
from jax import lax

IN_CHANNELS = 64
CHANNELS = 128
COLUMNS = 128
DEPTH1 = 64
HEIGHT1 = 64
COLUMNS2 = 64
DEPTH2 = 32
HEIGHT2 = 32
CELLS2 = 65536


def shard_levels(key, dims, split, low, high):
    def one(position, parts):
        heights = jax.random.uniform(jax.random.fold_in(jax.random.fold_in(key, 6), position), (parts,), jnp.float32, low / len(split), high / len(split))
        return jnp.repeat(jnp.exp(heights), dims[position] // parts).reshape((-1,) + (1,) * (len(dims) - position - 1))

    level = one(*split[0])
    for cut in split[1:]:
        level = level * one(*cut)
    return level


def normal_values(stream_key, dims, deviation, reach, cuts=(), kind=jnp.bfloat16):
    values = deviation * jax.random.normal(stream_key, dims, jnp.float32)
    if cuts:
        values = values * shard_levels(stream_key, dims, cuts, -0.22, 0.18)
    return jnp.clip(values, -reach, reach).astype(kind)


def setup_inputs(seed: int = 0) -> dict:
    arg_keys = jax.random.split(jax.random.key(seed), 5)
    volume = normal_values(arg_keys[0], (IN_CHANNELS, DEPTH1, HEIGHT1, COLUMNS), 1.0, 6.0, ((1, 32), (2, 16)))
    kernel_one = normal_values(arg_keys[1], (3, 3, 3, IN_CHANNELS, CHANNELS), (27 * IN_CHANNELS) ** -0.5, 0.15625)
    kernel_two = normal_values(arg_keys[2], (3, 3, 3, CHANNELS, CHANNELS), (27 * CHANNELS) ** -0.5, 0.109375)
    cotangent = normal_values(arg_keys[3], (CHANNELS, DEPTH2, HEIGHT2, COLUMNS2), 1.0, 6.0, ((0, 16), (1, 32)))
    return {"volume": volume, "kernel_one": kernel_one, "kernel_two": kernel_two, "cotangent": cotangent}


SLOPE = 0.2

def conv_local(inputs, kernel, stride, padding, dilation):
    result = lax.conv_general_dilated(inputs[None], kernel, window_strides=(stride, stride, stride), padding=padding, lhs_dilation=(dilation, dilation, dilation), dimension_numbers=('NCDHW', 'DHWIO', 'NCDHW'), preferred_element_type=jnp.float32)
    return result[0]

def flip_swap(kernel):
    return jnp.flip(kernel, (0, 1, 2)).transpose(0, 1, 2, 4, 3)

def weight_grad(padded, cotan, stride):
    cin = padded.shape[0]
    cout = cotan.shape[0]
    sizes = cotan.shape[1:]
    flat_cot = cotan.reshape(cout, -1)
    pieces = []
    for off_d in range(3):
        for off_h in range(3):
            for off_w in range(3):
                starts = (0, off_d, off_h, off_w)
                limits = (cin, off_d + stride * (sizes[0] - 1) + 1, off_h + stride * (sizes[1] - 1) + 1, off_w + stride * (sizes[2] - 1) + 1)
                window = lax.slice(padded, starts, limits, (1, stride, stride, stride))
                pieces.append(jnp.dot(window.reshape(cin, -1), flat_cot.T, preferred_element_type=jnp.float32))
    return jnp.stack(pieces).reshape(3, 3, 3, cin, cout)

def reference(volume, kernel_one, kernel_two, cotangent):
    zero3 = [(0, 0), (0, 0), (0, 0)]
    vol_pad = jnp.pad(volume, ((0, 0), (1, 0), (1, 0), (1, 0)))
    act_one = conv_local(vol_pad, kernel_one, 2, zero3, 1)
    hidden = (SLOPE * act_one + (1.0 - SLOPE) * jax.nn.softplus(act_one)).astype(jnp.bfloat16)
    hid_pad = jnp.pad(hidden, ((0, 0), (1, 1), (1, 1), (1, 1)))
    next_acts = conv_local(hid_pad, kernel_two, 1, zero3, 1).astype(jnp.bfloat16)
    cot_pad = jnp.pad(cotangent, ((0, 0), (1, 1), (1, 1), (1, 1)))
    hidden_grad = conv_local(cot_pad, flip_swap(kernel_two), 1, zero3, 1)
    act_grad = (hidden_grad * (SLOPE + (1.0 - SLOPE) * jax.nn.sigmoid(act_one))).astype(jnp.bfloat16)
    volume_grad = conv_local(act_grad, flip_swap(kernel_one), 1, [(1, 2), (1, 2), (1, 2)], 2).astype(jnp.bfloat16)
    scale = 1.0 / CELLS2 ** 0.5
    kernel_one_grad = weight_grad(vol_pad, act_grad, 2) * scale
    kernel_two_grad = weight_grad(hid_pad, cotangent, 1) * scale
    return (next_acts, volume_grad, kernel_one_grad, kernel_two_grad)
```

```python
import math

import jax
import jax.numpy as jnp
from jax import lax
from jax.sharding import Mesh, PartitionSpec as P

SLOPE = 0.2
DEPTH = ("x", "y", "zh")
HEIGHT = ("zl", "core")
PLANE = ("x", "y")
LINE = ("zh", "zl", "core")


def shifted(block, axis, distance):
    size = lax.axis_size(axis)
    route = [(i, i + distance) for i in range(size) if 0 <= i + distance < size]
    return lax.ppermute(block, axis, route)


def conv_local(inputs, kernel, stride, padding, dilation):
    result = lax.conv_general_dilated(
        inputs[None],
        kernel,
        window_strides=(stride, stride, stride),
        padding=padding,
        lhs_dilation=(dilation, dilation, dilation),
        dimension_numbers=("NCDHW", "DHWIO", "NCDHW"),
        preferred_element_type=jnp.float32,
    )
    return result[0]


def flip_swap(kernel):
    return jnp.flip(kernel, (0, 1, 2)).transpose(0, 1, 2, 4, 3)


def weight_grad(padded, cotan, stride):
    cin = padded.shape[0]
    cout = cotan.shape[0]
    sizes = cotan.shape[1:]
    flat_cot = cotan.reshape(cout, -1)
    pieces = []
    for off_d in range(3):
        for off_h in range(3):
            for off_w in range(3):
                starts = (0, off_d, off_h, off_w)
                limits = (
                    cin,
                    off_d + stride * (sizes[0] - 1) + 1,
                    off_h + stride * (sizes[1] - 1) + 1,
                    off_w + stride * (sizes[2] - 1) + 1,
                )
                window = lax.slice(padded, starts, limits, (1, stride, stride, stride))
                pieces.append(window.reshape(cin, -1))
    return lax.dot_general(
        jnp.stack(pieces),
        flat_cot,
        (((2,), (1,)), ((), ())),
        preferred_element_type=jnp.float32,
    )


def plane_sum(partial):
    taps, cin, cout = partial.shape
    parts = lax.axis_size(PLANE)
    sent = partial.astype(jnp.bfloat16).reshape(taps, parts, cin // parts, cout).transpose(1, 0, 2, 3)
    got = lax.all_to_all(sent, PLANE, 0, 0)
    return jnp.sum(got.astype(jnp.float32), axis=0)


def line_pieces(partial):
    taps, cin, cout = partial.shape
    far, near = (lax.axis_size("zh"), lax.axis_size(HEIGHT))
    cut = partial.reshape(taps, far, cin // far, near, cout // near)
    return cut.transpose(1, 3, 0, 2, 4).reshape(far * near, -1)


def per_device(volume, kernel_one, kernel_two, cotangent):
    zero3 = [(0, 0), (0, 0), (0, 0)]
    heights = lax.axis_size(HEIGHT)
    below = shifted(volume[:, -1:], DEPTH, 1)
    deeper = jnp.concatenate([below, volume], axis=1)
    beside = shifted(deeper[:, :, -1:], HEIGHT, 1)
    vol_pad = jnp.pad(jnp.concatenate([beside, deeper], axis=2), ((0, 0), (0, 0), (0, 0), (1, 0)))

    rows = cotangent.shape[2] // heights
    padded = jnp.pad(cotangent[:, 0], ((0, 0), (1, 1), (0, 0)))
    slabs = jnp.stack([padded[:, rows * i : rows * i + rows + 2] for i in range(heights)])
    slab = lax.all_to_all(slabs, HEIGHT, 0, 0)
    slab = slab.reshape((-1, 1) + slab.shape[2:])
    cot_ext = jnp.concatenate([shifted(slab, DEPTH, 1), slab, shifted(slab, DEPTH, -1)], axis=1)
    cot_ext = jnp.pad(cot_ext, ((0, 0), (0, 0), (0, 0), (1, 1)))
    cot_own = slab[:, :, 1:-1]

    act_one = conv_local(vol_pad, kernel_one, 2, zero3, 1)
    hidden = (SLOPE * act_one + (1.0 - SLOPE) * jax.nn.softplus(act_one)).astype(jnp.bfloat16)
    cells = (
        act_one.shape[1]
        * act_one.shape[2]
        * act_one.shape[3]
        * lax.axis_size(DEPTH)
        * lax.axis_size(HEIGHT)
    )
    scale = 1.0 / math.sqrt(cells)

    tall = jnp.concatenate(
        [shifted(hidden[:, :, -1:], HEIGHT, 1), hidden, shifted(hidden[:, :, :1], HEIGHT, -1)], axis=2
    )
    hid_ext = jnp.concatenate([shifted(tall, DEPTH, 1), tall, shifted(tall, DEPTH, -1)], axis=1)
    hid_pad = jnp.pad(hid_ext, ((0, 0), (0, 0), (0, 0), (1, 1)))

    own_next = conv_local(hid_pad, kernel_two, 1, zero3, 1).astype(jnp.bfloat16)
    groups = own_next.shape[0] // heights
    swapped = lax.all_to_all(own_next.reshape((heights, groups) + own_next.shape[1:]), HEIGHT, 0, 0)
    next_acts = swapped.transpose(1, 2, 0, 3, 4).reshape(cotangent.shape)

    two = plane_sum(weight_grad(hid_pad, cot_own, 1))

    hidden_grad = conv_local(cot_ext, flip_swap(kernel_two), 1, zero3, 1)
    act_grad = (hidden_grad * (SLOPE + (1.0 - SLOPE) * jax.nn.sigmoid(act_one))).astype(
        jnp.bfloat16
    )
    one = plane_sum(weight_grad(vol_pad, act_grad, 2))

    taller = jnp.concatenate([act_grad, shifted(act_grad[:, :, :1], HEIGHT, -1)], axis=2)
    grad_ext = jnp.concatenate([taller, shifted(taller, DEPTH, -1)], axis=1)
    volume_grad = conv_local(
        grad_ext, flip_swap(kernel_one), 1, [(1, 0), (1, 0), (1, 2)], 2
    ).astype(jnp.bfloat16)

    pieces = jnp.concatenate([line_pieces(one), line_pieces(two)], axis=1)
    total = jnp.sum(lax.all_to_all(pieces, LINE, 0, 0, tiled=True), axis=0) * scale
    line = lax.axis_size("zh")
    one_shape = (3, 3, 3, one.shape[1] // line, one.shape[2] // heights)
    two_shape = (3, 3, 3, two.shape[1] // line, two.shape[2] // heights)
    cut = math.prod(one_shape)
    return (next_acts, volume_grad, total[:cut].reshape(one_shape), total[cut:].reshape(two_shape))


def solution(mesh):
    fine = Mesh(mesh.devices.reshape(4, 4, 2, 8, 2), DEPTH + HEIGHT)
    placed = (P(None, DEPTH, HEIGHT, None), P(), P(), P(HEIGHT, DEPTH, None, None))
    return jax.shard_map(
        per_device,
        mesh=fine,
        in_specs=placed,
        out_specs=(
            P(HEIGHT, DEPTH, None, None),
            P(None, DEPTH, HEIGHT, None),
            P(None, None, None, DEPTH, HEIGHT),
            P(None, None, None, DEPTH, HEIGHT),
        ),
        check_vma=False,
    )
```

```python
import functools
import math

import jax
import jax.numpy as jnp
from jax import lax
from jax.experimental import pallas as pl
from jax.experimental.pallas import tpu as pltpu
from jax.sharding import Mesh, PartitionSpec as P

SLOPE = 0.2
DEPTH = ("x", "y", "zh")
HEIGHT = ("zl", "core")
PLANE = ("x", "y")
LINE = ("zh", "zl", "core")
BF = jnp.bfloat16
F32 = jnp.float32
PAIRS = tuple((a, b) for a in range(3) for b in range(3))


def dot(a, b, ca=1, cb=0):
    return lax.dot_general(a, b, (((ca,), (cb,)), ((), ())), preferred_element_type=F32)


def iota(shape, dim):
    return lax.broadcasted_iota(jnp.int32, shape, dim)


def one_hot(mask):
    return jnp.where(mask, 1.0, 0.0).astype(BF)


def earlier(x):
    return jnp.where(iota(x.shape, 0) % 64 == 0, 0.0, pltpu.roll(x, 1, 0))


def later(x):
    return jnp.where(iota(x.shape, 0) % 64 == 63, 0.0, pltpu.roll(x, x.shape[0] - 1, 0))


def call(body, outs, *args, scalars=0):
    smem = pl.BlockSpec(memory_space=pltpu.SMEM)
    vmem = pl.BlockSpec(memory_space=pltpu.VMEM)
    many = isinstance(outs, list)
    return pl.pallas_call(
        body,
        out_shape=outs,
        in_specs=[smem] * scalars + [vmem] * (len(args) - scalars),
        out_specs=[vmem] * len(outs) if many else vmem,
        compiler_params=pltpu.CompilerParams(vmem_limit_bytes=48 * 1024 * 1024),
    )(*args)


def prep_body(vol_ref, cot_ref, volt_ref, slab_ref):
    shape = (512, 512)
    to, of = iota(shape, 0), iota(shape, 1)
    rows = dot(one_hot(of == (to % 64) * 8 + to // 64), vol_ref[...]).astype(BF)
    half = (64, 128)
    even = one_hot(iota(half, 1) == 2 * iota(half, 0))
    odd = one_hot(iota(half, 1) == 2 * iota(half, 0) + 1)
    zero = jnp.zeros((64, 128), BF)
    for i in range(8):
        block = rows[64 * i : 64 * i + 64]
        left = jnp.concatenate([block, zero], axis=0)
        right = jnp.concatenate([zero, block], axis=0)
        volt_ref[i // 4, i % 4] = (dot(even, left, 1, 1) + dot(odd, right, 1, 1)).astype(BF)
    for i in range(16):
        for j in range(3):
            pair = i + j - 1
            if 0 <= pair < 16:
                piece = cot_ref[:, 128 * pair : 128 * pair + 128]
            else:
                piece = jnp.zeros((8, 128), BF)
            slab_ref[i, :, 128 * j : 128 * j + 128] = piece
            slab_ref[16 + i, :, 128 * j : 128 * j + 128] = piece


def turn_body(got_ref, out_ref):
    eye = one_hot(iota((128, 128), 0) == iota((128, 128), 1))
    for q in range(2):
        for j in range(3):
            block = got_ref[128 * q : 128 * q + 128, 128 * j : 128 * j + 128]
            turned = dot(eye, block, 1, 1).astype(BF)
            out_ref[q, 2 * j] = turned[:64]
            out_ref[q, 2 * j + 1] = turned[64:]


def conv_one_body(h_ref, v_ref, k_ref, act_ref, hid_ref):
    acc = jnp.zeros((512, 256), F32)
    for i, (a, b) in enumerate(PAIRS):
        x = jnp.concatenate([v_ref[2 * q + a, 2 * r + b] for q in range(2) for r in range(4)], axis=0)
        taps = k_ref[i]
        right = jnp.concatenate([jnp.zeros((64, 128), BF), taps[:64]], axis=0)
        acc += dot(x, jnp.concatenate([taps[64:], right], axis=1))
    act = acc[:, :128] + earlier(acc[:, 128:])
    soft = jnp.maximum(act, 0.0) + jnp.log1p(jnp.exp(-jnp.abs(act)))
    hidden = SLOPE * act + (1.0 - SLOPE) * soft
    row = iota((512, 128), 0) // 64 % 4 + 2 * h_ref[0] - 1
    hidden = jnp.where((row >= 0) & (row < 32), hidden, 0.0).astype(BF)
    for q in range(2):
        for r in range(4):
            at = 64 * (4 * q + r)
            act_ref[q, r] = act[at : at + 64]
            hid_ref[q, r] = hidden[at : at + 64]


def grads_body(s_ref, c_ref, k_ref, act_ref, hid_ref, v_ref, ag_ref, out_ref):
    h, zh = s_ref[0], s_ref[1]
    acc = jnp.zeros((384, 384), F32)
    for a, b in PAIRS:
        x = jnp.concatenate(
            [c_ref[q + a, r + 1 + b] for q in range(2) for r in range(3)], axis=0
        )
        acc += dot(x, k_ref[3 * (2 - a) + 2 - b], 1, 1)
    grad = acc[:, 128:256] + earlier(acc[:, 256:]) + later(acc[:, :128])
    act = jnp.concatenate([act_ref[q, r + 1] for q in range(2) for r in range(3)], axis=0)
    small = jnp.exp(-jnp.abs(act))
    sigmoid = jnp.where(act >= 0.0, 1.0, small) / (1.0 + small)
    grad = grad * (SLOPE + (1.0 - SLOPE) * sigmoid)
    row = iota((384, 128), 0) // 64 % 3 + 2 * h
    ag = jnp.where(row < 32, grad, 0.0).astype(BF)
    for q in range(2):
        for r in range(3):
            at = 64 * (3 * q + r)
            ag_ref[q, r] = ag[at : at + 64]
    own_ag = jnp.concatenate([ag[:128], ag[192:320]], axis=0)

    lane = iota((128, 256), 1)
    source = iota((128, 256), 0)
    device, slot = lane // 16, lane % 16
    pick_two = one_hot((slot < 12) & (source == device * 8 + zh * 4 + slot % 4))
    own_hid = jnp.concatenate([hid_ref[q, r + 1] for q in range(2) for r in range(2)], axis=0)
    flat = dot(own_hid, pick_two)
    tap = iota((256, 256), 1) % 16 // 4
    hid_rows = jnp.where(tap == 0, earlier(flat), jnp.where(tap == 1, flat, later(flat))).astype(BF)
    pick_one = one_hot(
        (slot >= 12) & (source == (slot - 12) // 2 * 64 + device * 4 + zh * 2 + slot % 2)
    )
    first = jnp.zeros((256, 256), F32)
    last = None
    for i, (a, b) in enumerate(PAIRS):
        x = jnp.concatenate(
            [v_ref[2 * q + a, 2 * r + 2 + b] for q in range(2) for r in range(2)], axis=0
        )
        vol_rows = dot(x, pick_one).astype(BF)
        cot = jnp.concatenate(
            [c_ref[q + 2 - a, r + 3 - b] for q in range(2) for r in range(2)], axis=0
        )
        both = dot(hid_rows, cot, 0, 0) + dot(vol_rows, own_ag, 0, 0)
        out_ref[:, :, 128 * i : 128 * i + 128] = both.astype(BF).reshape(16, 16, 128)
        here = one_hot(
            (slot // 2 == i % 8) & (source == 64 + device * 4 + zh * 2 + slot % 2)
        )
        picked = dot(x, here)
        if i < 8:
            first += picked
        else:
            last = picked
    for i, rows in ((9, first), (10, last)):
        part = dot(earlier(rows).astype(BF), own_ag, 0, 0)
        out_ref[:, :, 128 * i : 128 * i + 128] = part.astype(BF).reshape(16, 16, 128)


def conv_two_body(h_ref, k_ref, out_ref):
    acc = jnp.zeros((128, 128), F32)
    for i, (a, b) in enumerate(PAIRS):
        x = jnp.concatenate([h_ref[a, b], h_ref[a, b + 1]], axis=0)
        wide = x.astype(F32)
        taps = jnp.concatenate([earlier(wide).astype(BF), x, later(wide).astype(BF)], axis=1)
        acc += dot(taps, k_ref[i])
    out_ref[...] = acc.T.astype(BF)


def volume_grad_body(a_ref, k_ref, out_ref):
    zero = jnp.zeros((64, 128), BF)
    half = (64, 256)
    spread = one_hot(iota(half, 1) % 128 == 2 * iota(half, 0) + iota(half, 1) // 128)
    offsets = (((1, 0),), ((0, 1), (2, 0)))
    blocks = [None] * 8
    for pi in range(2):
        for pj in range(2):
            acc = jnp.zeros((128, 256), F32)
            for a, plane in offsets[pi]:
                for b, row in offsets[pj]:
                    x = jnp.concatenate([a_ref[plane, row], a_ref[plane, row + 1]], axis=0)
                    taps = k_ref[3 * a + b]
                    weights = jnp.concatenate([taps[64:], zero, taps[:64]], axis=0)
                    acc += dot(x, weights, 1, 1)
            cells = (acc[:, :128] + later(acc[:, 128:])).astype(BF)
            for r in range(2):
                wide = dot(cells[64 * r : 64 * r + 64], spread, 0, 0)
                blocks[4 * pi + 2 * r + pj] = (wide[:64, :128] + wide[64:, 128:]).astype(BF)
    shape = (512, 512)
    to, of = iota(shape, 0), iota(shape, 1)
    turn = one_hot(of == (to % 8) * 64 + to // 8)
    out_ref[...] = dot(turn, jnp.concatenate(blocks, axis=0)).astype(BF)


def plane_sum_body(got_ref, out_ref):
    total = got_ref[0].astype(F32)
    for i in range(1, 16):
        total += got_ref[i].astype(F32)
    pieces = [total[:, 128 * j : 128 * j + 128] for j in range(11)]
    rows = jnp.concatenate(pieces + [jnp.zeros((80, 128), F32)], axis=0)
    out_ref[...] = rows.T


def line_sum_body(scale, got_ref, out_ref):
    total = got_ref[0]
    for i in range(1, 16):
        total += got_ref[i]
    out_ref[...] = total * scale


def shifted(block, axis, distance):
    size = lax.axis_size(axis)
    route = [(i, i + distance) for i in range(size) if 0 <= i + distance < size]
    return lax.ppermute(block, axis, route)


def shape(dims, kind=BF):
    return jax.ShapeDtypeStruct(dims, kind)


def per_device(volume, kernel_one, kernel_two, cotangent):
    zh = lax.axis_index("zh")
    h = lax.axis_index(HEIGHT)
    here = jnp.stack([h, zh]).astype(jnp.int32)
    one = kernel_one.reshape(9, 192, 128)
    two = kernel_two.reshape(9, 384, 128)
    planes = lax.axis_size(PLANE)

    own, slabs = call(
        prep_body,
        [shape((2, 4, 64, 128)), shape((32, 8, 384))],
        volume.reshape(512, 128),
        cotangent.reshape(8, 2048),
    )
    other = lax.ppermute(own, "zh", [(0, 1), (1, 0)])
    slab = lax.all_to_all(slabs, LINE, 0, 0, tiled=True)
    low = jnp.where(zh == 0, own, other)
    high = jnp.where(zh == 0, other, own)
    deep = jnp.concatenate([shifted(high[1:], PLANE, 1), low, high], axis=0)
    vol = jnp.concatenate(
        [shifted(deep[:, 1:], HEIGHT, 1), deep, shifted(deep[:, :2], HEIGHT, -1)], axis=1
    )
    cot = call(turn_body, shape((2, 6, 64, 128)), slab.reshape(256, 384))
    cot = jnp.concatenate([shifted(cot[1:], PLANE, 1), cot, shifted(cot[:1], PLANE, -1)], axis=0)

    act, hidden = call(
        conv_one_body,
        [shape((2, 4, 64, 128), F32), shape((2, 4, 64, 128))],
        here,
        vol,
        one,
        scalars=1,
    )
    ag, partial = call(
        grads_body,
        [shape((2, 3, 64, 128)), shape((16, 16, 1408))],
        here,
        cot,
        two,
        act,
        hidden,
        vol,
        scalars=1,
    )
    parts = lax.all_to_all(partial, PLANE, 0, 0, tiled=True)

    up = [(2 * k, 2 * k + 2) for k in range(planes - 1)]
    down = [(2 * k + 1, 2 * k - 1) for k in range(1, planes)]
    edge = lax.ppermute(jnp.where(zh == 0, hidden[1:], hidden[:1]), DEPTH, up + down)
    three = jnp.where(
        zh == 0, jnp.concatenate([edge, hidden], axis=0), jnp.concatenate([hidden, edge], axis=0)
    )
    next_own = call(conv_two_body, shape((128, 128)), three, two)
    swapped = lax.all_to_all(next_own.reshape(16, 8, 128), HEIGHT, 0, 0, tiled=True)
    next_acts = swapped.reshape(16, 8, 2, 64).transpose(1, 0, 2, 3).reshape(cotangent.shape)

    after = lax.ppermute(ag[:1], DEPTH, down)
    pair = jnp.where(zh == 0, ag, jnp.concatenate([ag[1:], after], axis=0))
    volume_grad = call(volume_grad_body, shape((512, 128)), pair, one).reshape(volume.shape)

    summed = call(plane_sum_body, shape((128, 256), F32), parts)
    rows = lax.all_to_all(summed.reshape(16, 8, 256), HEIGHT, 0, 0, tiled=True)
    total = call(functools.partial(line_sum_body, 1.0 / math.sqrt(65536)), shape((8, 256), F32), rows)
    table = total.T
    slots = table[:144].reshape(9, 16, 8)
    two_grad = slots[:, :12].reshape(3, 3, 3, 4, 8)
    before = table[144:162].reshape(9, 1, 2, 8)
    one_grad = jnp.concatenate([before, slots[:, 12:].reshape(9, 2, 2, 8)], axis=1)
    return (next_acts, volume_grad, one_grad.reshape(3, 3, 3, 2, 8), two_grad)


def solution(mesh):
    fine = Mesh(mesh.devices.reshape(4, 4, 2, 8, 2), DEPTH + HEIGHT)
    placed = (P(None, DEPTH, HEIGHT, None), P(), P(), P(HEIGHT, DEPTH, None, None))
    return jax.shard_map(
        per_device,
        mesh=fine,
        in_specs=placed,
        out_specs=(
            P(HEIGHT, DEPTH, None, None),
            P(None, DEPTH, HEIGHT, None),
            P(None, None, None, DEPTH, HEIGHT),
            P(None, None, None, DEPTH, HEIGHT),
        ),
        check_vma=False,
    )
```

```python
import functools
import math

import jax
import jax.numpy as jnp
from jax import lax
from jax.experimental import pallas as pl
from jax.experimental.pallas import tpu as pltpu
from jax.sharding import Mesh, PartitionSpec as P

SLOPE = 0.2
DEPTH = ("x", "y", "zh")
HEIGHT = ("zl", "core")
PLANE = ("x", "y")
LINE = ("zh", "zl", "core")
BF = jnp.bfloat16
F32 = jnp.float32
PAIRS = tuple((a, b) for a in range(3) for b in range(3))


def dot(a, b, ca=1, cb=0):
    return lax.dot_general(a, b, (((ca,), (cb,)), ((), ())), preferred_element_type=F32)


def iota(shape, dim):
    return lax.broadcasted_iota(jnp.int32, shape, dim)


def one_hot(mask):
    return jnp.where(mask, 1.0, 0.0).astype(BF)


def earlier(x):
    return jnp.where(iota(x.shape, 0) % 64 == 0, 0.0, pltpu.roll(x, 1, 0))


def later(x):
    return jnp.where(iota(x.shape, 0) % 64 == 63, 0.0, pltpu.roll(x, x.shape[0] - 1, 0))


def call(body, outs, *args, scalars=0):
    smem = pl.BlockSpec(memory_space=pltpu.SMEM)
    vmem = pl.BlockSpec(memory_space=pltpu.VMEM)
    many = isinstance(outs, list)
    return pl.pallas_call(
        body,
        out_shape=outs,
        in_specs=[smem] * scalars + [vmem] * (len(args) - scalars),
        out_specs=[vmem] * len(outs) if many else vmem,
        compiler_params=pltpu.CompilerParams(vmem_limit_bytes=48 * 1024 * 1024),
    )(*args)


def columns_body(vol_ref, out_ref):
    shape = (512, 512)
    to, of = iota(shape, 0), iota(shape, 1)
    rows = dot(one_hot(of == (to % 64) * 8 + to // 64), vol_ref[...]).astype(BF)
    half = (64, 128)
    even = one_hot(iota(half, 1) == 2 * iota(half, 0))
    odd = one_hot(iota(half, 1) == 2 * iota(half, 0) + 1)
    zero = jnp.zeros((64, 128), BF)
    for i in range(8):
        block = rows[64 * i : 64 * i + 64]
        left = jnp.concatenate([block, zero], axis=0)
        right = jnp.concatenate([zero, block], axis=0)
        out_ref[i // 4, i % 4] = (dot(even, left, 1, 1) + dot(odd, right, 1, 1)).astype(BF)


def slabs_body(cot_ref, after_ref, slab_ref):
    del after_ref
    for i in range(16):
        for j in range(3):
            pair = i + j - 1
            if 0 <= pair < 16:
                piece = cot_ref[:, 128 * pair : 128 * pair + 128]
            else:
                piece = jnp.zeros((8, 128), BF)
            slab_ref[i, :, 128 * j : 128 * j + 128] = piece
            slab_ref[16 + i, :, 128 * j : 128 * j + 128] = piece


def turn_body(got_ref, out_ref):
    eye = one_hot(iota((128, 128), 0) == iota((128, 128), 1))
    for q in range(2):
        for j in range(3):
            block = got_ref[128 * q : 128 * q + 128, 128 * j : 128 * j + 128]
            turned = dot(eye, block, 1, 1).astype(BF)
            out_ref[q, 2 * j] = turned[:64]
            out_ref[q, 2 * j + 1] = turned[64:]


def conv_one_body(h_ref, v_ref, k_ref, act_ref, hid_ref):
    cells, weights = [], []
    for i, (a, b) in enumerate(PAIRS):
        rows = [v_ref[2 * q + a, 2 * r + b] for q in range(2) for r in range(4)]
        cells.append(jnp.concatenate(rows, axis=0))
        taps = k_ref[i]
        right = jnp.concatenate([jnp.zeros((64, 128), BF), taps[:64]], axis=0)
        weights.append(jnp.concatenate([taps[64:], right], axis=1))
    acc = dot(jnp.concatenate(cells, axis=1), jnp.concatenate(weights, axis=0))
    act = acc[:, :128] + earlier(acc[:, 128:])
    soft = jnp.maximum(act, 0.0) + jnp.log1p(jnp.exp(-jnp.abs(act)))
    hidden = SLOPE * act + (1.0 - SLOPE) * soft
    row = iota((512, 128), 0) // 64 % 4 + 2 * h_ref[0] - 1
    hidden = jnp.where((row >= 0) & (row < 32), hidden, 0.0).astype(BF)
    for q in range(2):
        for r in range(4):
            at = 64 * (4 * q + r)
            act_ref[q, r] = act[at : at + 64]
            hid_ref[q, r] = hidden[at : at + 64]


def grads_body(s_ref, c_ref, k_ref, act_ref, hid_ref, v_ref, ag_ref, out_ref):
    h, zh = s_ref[0], s_ref[1]
    cells, weights = [], []
    for a, b in PAIRS:
        rows = [c_ref[q + a, r + 1 + b] for q in range(2) for r in range(3)]
        cells.append(jnp.concatenate(rows, axis=0))
        weights.append(k_ref[3 * (2 - a) + 2 - b])
    acc = dot(jnp.concatenate(cells, axis=1), jnp.concatenate(weights, axis=1), 1, 1)
    grad = acc[:, 128:256] + earlier(acc[:, 256:]) + later(acc[:, :128])
    act = jnp.concatenate([act_ref[q, r + 1] for q in range(2) for r in range(3)], axis=0)
    small = jnp.exp(-jnp.abs(act))
    sigmoid = jnp.where(act >= 0.0, 1.0, small) / (1.0 + small)
    grad = grad * (SLOPE + (1.0 - SLOPE) * sigmoid)
    row = iota((384, 128), 0) // 64 % 3 + 2 * h
    ag = jnp.where(row < 32, grad, 0.0).astype(BF)
    for q in range(2):
        for r in range(3):
            at = 64 * (3 * q + r)
            ag_ref[q, r] = ag[at : at + 64]
    own_ag = jnp.concatenate([ag[:128], ag[192:320]], axis=0)

    slot_row = iota((256, 128), 0)
    source = iota((256, 128), 1)
    device, slot = slot_row // 16, slot_row % 16
    pick_two = one_hot((slot < 12) & (source == device * 8 + zh * 4 + slot % 4))
    own_hid = jnp.concatenate([hid_ref[q, r + 1] for q in range(2) for r in range(2)], axis=0)
    flat = dot(pick_two, own_hid, 1, 1)
    tap = iota((256, 256), 0) % 16 // 4
    column = iota((256, 256), 1) % 64
    before = jnp.where(column == 0, 0.0, pltpu.roll(flat, 1, 1))
    after = jnp.where(column == 63, 0.0, pltpu.roll(flat, 255, 1))
    hid_rows = jnp.where(tap == 0, before, jnp.where(tap == 1, flat, after)).astype(BF)
    cots = [
        jnp.concatenate([c_ref[q + 2 - a, r + 3 - b] for q in range(2) for r in range(2)], axis=0)
        for a, b in PAIRS
    ]
    first = dot(hid_rows, jnp.concatenate(cots, axis=1))
    channel = device * 4 + zh * 2 + slot % 2
    pick_one = one_hot((slot >= 12) & (source == (slot - 12) // 2 * 64 + channel))
    vols, picks = [], []
    for i, (a, b) in enumerate(PAIRS):
        x = jnp.concatenate(
            [v_ref[2 * q + a, 2 * r + 2 + b] for q in range(2) for r in range(2)], axis=0
        )
        vol_rows = dot(pick_one, x, 1, 1).astype(BF)
        both = first[:, 128 * i : 128 * i + 128] + dot(vol_rows, own_ag)
        out_ref[:, :, 128 * i : 128 * i + 128] = both.astype(BF).reshape(16, 16, 128)
        vols.append(x)
        picks.append(one_hot((slot // 2 == i % 8) & (source == 64 + channel)))
    groups = (
        (9, jnp.concatenate(picks[:8], axis=1), jnp.concatenate(vols[:8], axis=1)),
        (10, picks[8], vols[8]),
    )
    for i, pick, x in groups:
        rows = dot(pick, x, 1, 1)
        rows = jnp.where(column == 0, 0.0, pltpu.roll(rows, 1, 1)).astype(BF)
        out_ref[:, :, 128 * i : 128 * i + 128] = dot(rows, own_ag).astype(BF).reshape(16, 16, 128)


def conv_two_body(h_ref, k_ref, out_ref):
    cells = []
    for a, b in PAIRS:
        x = jnp.concatenate([h_ref[a, b], h_ref[a, b + 1]], axis=0)
        wide = x.astype(F32)
        cells += [earlier(wide).astype(BF), x, later(wide).astype(BF)]
    acc = dot(jnp.concatenate(cells, axis=1), k_ref[...])
    out_ref[...] = acc.T.astype(BF)


def volume_grad_body(a_ref, k_ref, out_ref):
    zero = jnp.zeros((64, 128), BF)
    half = (64, 256)
    spread = one_hot(iota(half, 1) % 128 == 2 * iota(half, 0) + iota(half, 1) // 128)
    offsets = (((1, 0),), ((0, 1), (2, 0)))
    blocks = [None] * 8
    for pi in range(2):
        for pj in range(2):
            acc = jnp.zeros((128, 256), F32)
            for a, plane in offsets[pi]:
                for b, row in offsets[pj]:
                    x = jnp.concatenate([a_ref[plane, row], a_ref[plane, row + 1]], axis=0)
                    taps = k_ref[3 * a + b]
                    weights = jnp.concatenate([taps[64:], zero, taps[:64]], axis=0)
                    acc += dot(x, weights, 1, 1)
            cells = (acc[:, :128] + later(acc[:, 128:])).astype(BF)
            for r in range(2):
                wide = dot(cells[64 * r : 64 * r + 64], spread, 0, 0)
                blocks[4 * pi + 2 * r + pj] = (wide[:64, :128] + wide[64:, 128:]).astype(BF)
    shape = (512, 512)
    to, of = iota(shape, 0), iota(shape, 1)
    turn = one_hot(of == (to % 8) * 64 + to // 8)
    out_ref[...] = dot(turn, jnp.concatenate(blocks, axis=0)).astype(BF)


def plane_sum_body(got_ref, next_ref, out_ref):
    total = got_ref[0].astype(F32)
    for i in range(1, 16):
        total += got_ref[i].astype(F32)
    pieces = [total[:, 128 * j : 128 * j + 128] for j in range(11)]
    rows = jnp.concatenate(pieces + [jnp.zeros((80, 128), F32)], axis=0)
    out_ref[:, :128] = next_ref[...]
    out_ref[:, 128:] = rows.T.astype(BF)


def line_sum_body(scale, got_ref, out_ref):
    total = got_ref[0].astype(F32)
    for i in range(1, 16):
        total += got_ref[i].astype(F32)
    out_ref[...] = (total[:, 128:] * scale).T


def shifted(block, axis, distance):
    size = lax.axis_size(axis)
    route = [(i, i + distance) for i in range(size) if 0 <= i + distance < size]
    return lax.ppermute(block, axis, route)


def shape(dims, kind=BF):
    return jax.ShapeDtypeStruct(dims, kind)


def per_device(volume, kernel_one, kernel_two, cotangent):
    zh = lax.axis_index("zh")
    h = lax.axis_index(HEIGHT)
    here = jnp.stack([h, zh]).astype(jnp.int32)
    one = kernel_one.reshape(9, 192, 128)
    two = kernel_two.reshape(9, 384, 128)
    planes = lax.axis_size(PLANE)

    own = call(columns_body, shape((2, 4, 64, 128)), volume.reshape(512, 128))
    slabs = call(slabs_body, shape((32, 8, 384)), cotangent.reshape(8, 2048), own)
    other = lax.ppermute(own, "zh", [(0, 1), (1, 0)])
    slab = lax.all_to_all(slabs, LINE, 0, 0, tiled=True)
    low = jnp.where(zh == 0, own, other)
    high = jnp.where(zh == 0, other, own)
    deep = jnp.concatenate([shifted(high[1:], PLANE, 1), low, high], axis=0)
    vol = jnp.concatenate(
        [shifted(deep[:, 1:], HEIGHT, 1), deep, shifted(deep[:, :2], HEIGHT, -1)], axis=1
    )
    cot = call(turn_body, shape((2, 6, 64, 128)), slab.reshape(256, 384))
    cot = jnp.concatenate([shifted(cot[1:], PLANE, 1), cot, shifted(cot[:1], PLANE, -1)], axis=0)

    act, hidden = call(
        conv_one_body,
        [shape((2, 4, 64, 128), F32), shape((2, 4, 64, 128))],
        here,
        vol,
        one,
        scalars=1,
    )
    up = [(2 * k, 2 * k + 2) for k in range(planes - 1)]
    down = [(2 * k + 1, 2 * k - 1) for k in range(1, planes)]
    edge = lax.ppermute(jnp.where(zh == 0, hidden[1:], hidden[:1]), DEPTH, up + down)
    edge, cot = lax.optimization_barrier((edge, cot))
    ag, partial = call(
        grads_body,
        [shape((2, 3, 64, 128)), shape((16, 16, 1408))],
        here,
        cot,
        two,
        act,
        hidden,
        vol,
        scalars=1,
    )
    parts = lax.all_to_all(partial, PLANE, 0, 0, tiled=True)
    three = jnp.where(
        zh == 0, jnp.concatenate([edge, hidden], axis=0), jnp.concatenate([hidden, edge], axis=0)
    )
    next_own = call(conv_two_body, shape((128, 128)), three, kernel_two.reshape(3456, 128))

    after = lax.ppermute(ag[:1], DEPTH, down)
    pair = jnp.where(zh == 0, ag, jnp.concatenate([ag[1:], after], axis=0))
    volume_grad = call(volume_grad_body, shape((512, 128)), pair, one).reshape(volume.shape)

    summed = call(plane_sum_body, shape((128, 384)), parts, next_own)
    rows = lax.all_to_all(summed.reshape(16, 8, 384), HEIGHT, 0, 0, tiled=True)
    swapped = rows[:, :, :128].reshape(16, 8, 2, 64)
    next_acts = swapped.transpose(1, 0, 2, 3).reshape(cotangent.shape)
    table = call(functools.partial(line_sum_body, 1.0 / math.sqrt(65536)), shape((256, 8), F32), rows)
    slots = table[:144].reshape(9, 16, 8)
    two_grad = slots[:, :12].reshape(3, 3, 3, 4, 8)
    before = table[144:162].reshape(9, 1, 2, 8)
    one_grad = jnp.concatenate([before, slots[:, 12:].reshape(9, 2, 2, 8)], axis=1)
    return (next_acts, volume_grad, one_grad.reshape(3, 3, 3, 2, 8), two_grad)


def solution(mesh):
    fine = Mesh(mesh.devices.reshape(4, 4, 2, 8, 2), DEPTH + HEIGHT)
    placed = (P(None, DEPTH, HEIGHT, None), P(), P(), P(HEIGHT, DEPTH, None, None))
    return jax.shard_map(
        per_device,
        mesh=fine,
        in_specs=placed,
        out_specs=(
            P(HEIGHT, DEPTH, None, None),
            P(None, DEPTH, HEIGHT, None),
            P(None, None, None, DEPTH, HEIGHT),
            P(None, None, None, DEPTH, HEIGHT),
        ),
        check_vma=False,
    )
```

```python
import functools
import math

import jax
import jax.numpy as jnp
from jax import lax
from jax.experimental import pallas as pl
from jax.experimental.pallas import tpu as pltpu
from jax.sharding import Mesh, PartitionSpec as P

SLOPE = 0.2
DEPTH = ("x", "y", "zh")
HEIGHT = ("zl", "core")
PLANE = ("x", "y")
LINE = ("zh", "zl", "core")
BF = jnp.bfloat16
F32 = jnp.float32
PAIRS = tuple((a, b) for a in range(3) for b in range(3))


def dot(a, b, ca=1, cb=0):
    return lax.dot_general(a, b, (((ca,), (cb,)), ((), ())), preferred_element_type=F32)


def iota(shape, dim):
    return lax.broadcasted_iota(jnp.int32, shape, dim)


def one_hot(mask):
    return jnp.where(mask, 1.0, 0.0).astype(BF)


def earlier(x):
    return jnp.where(iota(x.shape, 0) % 64 == 0, 0.0, pltpu.roll(x, 1, 0))


def later(x):
    return jnp.where(iota(x.shape, 0) % 64 == 63, 0.0, pltpu.roll(x, x.shape[0] - 1, 0))


def call(body, outs, *args, scalars=0, flops=0):
    smem = pl.BlockSpec(memory_space=pltpu.SMEM)
    vmem = pl.BlockSpec(memory_space=pltpu.VMEM)
    many = isinstance(outs, list)
    return pl.pallas_call(
        body,
        out_shape=outs,
        in_specs=[smem] * scalars + [vmem] * (len(args) - scalars),
        out_specs=[vmem] * len(outs) if many else vmem,
        compiler_params=pltpu.CompilerParams(vmem_limit_bytes=48 * 1024 * 1024),
        cost_estimate=pl.CostEstimate(flops=flops, bytes_accessed=0, transcendentals=0) if flops else None,
    )(*args)


def columns_body(vol_ref, out_ref):
    shape = (512, 512)
    to, of = iota(shape, 0), iota(shape, 1)
    rows = dot(one_hot(of == (to % 64) * 8 + to // 64), vol_ref[...]).astype(BF)
    half = (64, 128)
    even = one_hot(iota(half, 1) == 2 * iota(half, 0))
    odd = one_hot(iota(half, 1) == 2 * iota(half, 0) + 1)
    zero = jnp.zeros((64, 128), BF)
    for i in range(8):
        block = rows[64 * i : 64 * i + 64]
        left = jnp.concatenate([block, zero], axis=0)
        right = jnp.concatenate([zero, block], axis=0)
        out_ref[i // 4, i % 4] = (dot(even, left, 1, 1) + dot(odd, right, 1, 1)).astype(BF)


def slabs_body(cot_ref, after_ref, slab_ref):
    del after_ref
    for i in range(16):
        for j in range(3):
            pair = i + j - 1
            if 0 <= pair < 16:
                piece = cot_ref[:, 128 * pair : 128 * pair + 128]
            else:
                piece = jnp.zeros((8, 128), BF)
            slab_ref[i, :, 128 * j : 128 * j + 128] = piece
            slab_ref[16 + i, :, 128 * j : 128 * j + 128] = piece


def order_body(s_ref, own_ref, other_ref, out_ref):
    first = s_ref[1]
    for i in range(2):
        out_ref[2 * first + i] = own_ref[i]
        out_ref[2 - 2 * first + i] = other_ref[i]


def turn_body(got_ref, out_ref):
    eye = one_hot(iota((128, 128), 0) == iota((128, 128), 1))
    for q in range(2):
        for j in range(3):
            block = got_ref[128 * q : 128 * q + 128, 128 * j : 128 * j + 128]
            turned = dot(eye, block, 1, 1).astype(BF)
            out_ref[q, 2 * j] = turned[:64]
            out_ref[q, 2 * j + 1] = turned[64:]


def conv_one_body(h_ref, v_ref, k_ref, act_ref, hid_ref):
    cells, weights = [], []
    for i, (a, b) in enumerate(PAIRS):
        rows = [v_ref[2 * q + a, 2 * r + b] for q in range(2) for r in range(4)]
        cells.append(jnp.concatenate(rows, axis=0))
        taps = k_ref[i]
        right = jnp.concatenate([jnp.zeros((64, 128), BF), taps[:64]], axis=0)
        weights.append(jnp.concatenate([taps[64:], right], axis=1))
    acc = dot(jnp.concatenate(cells, axis=1), jnp.concatenate(weights, axis=0))
    act = acc[:, :128] + earlier(acc[:, 128:])
    soft = jnp.maximum(act, 0.0) + jnp.log1p(jnp.exp(-jnp.abs(act)))
    hidden = SLOPE * act + (1.0 - SLOPE) * soft
    row = iota((512, 128), 0) // 64 % 4 + 2 * h_ref[0] - 1
    hidden = jnp.where((row >= 0) & (row < 32), hidden, 0.0).astype(BF)
    for q in range(2):
        for r in range(4):
            at = 64 * (4 * q + r)
            act_ref[q, r] = act[at : at + 64]
            hid_ref[q, r] = hidden[at : at + 64]


def hidden_grad_body(s_ref, c_ref, k_ref, act_ref, ag_ref):
    h = s_ref[0]
    cells, weights = [], []
    for a, b in PAIRS:
        rows = [c_ref[q + a, r + 1 + b] for q in range(2) for r in range(3)]
        cells.append(jnp.concatenate(rows, axis=0))
        weights.append(k_ref[3 * (2 - a) + 2 - b])
    acc = dot(jnp.concatenate(cells, axis=1), jnp.concatenate(weights, axis=1), 1, 1)
    grad = acc[:, 128:256] + earlier(acc[:, 256:]) + later(acc[:, :128])
    act = jnp.concatenate([act_ref[q, r + 1] for q in range(2) for r in range(3)], axis=0)
    small = jnp.exp(-jnp.abs(act))
    sigmoid = jnp.where(act >= 0.0, 1.0, small) / (1.0 + small)
    grad = grad * (SLOPE + (1.0 - SLOPE) * sigmoid)
    row = iota((384, 128), 0) // 64 % 3 + 2 * h
    ag = jnp.where(row < 32, grad, 0.0).astype(BF)
    for q in range(2):
        for r in range(3):
            at = 64 * (3 * q + r)
            ag_ref[q, r] = ag[at : at + 64]


def kernel_grads_body(s_ref, c_ref, ag_ref, hid_ref, v_ref, out_ref):
    zh = s_ref[1]
    own_ag = jnp.concatenate([ag_ref[q, r] for q in range(2) for r in range(2)], axis=0)
    slot_row = iota((256, 128), 0)
    source = iota((256, 128), 1)
    device, slot = slot_row // 16, slot_row % 16
    pick_two = one_hot((slot < 12) & (source == device * 8 + zh * 4 + slot % 4))
    own_hid = jnp.concatenate([hid_ref[q, r + 1] for q in range(2) for r in range(2)], axis=0)
    flat = dot(pick_two, own_hid, 1, 1)
    tap = iota((256, 256), 0) % 16 // 4
    column = iota((256, 256), 1) % 64
    before = jnp.where(column == 0, 0.0, pltpu.roll(flat, 1, 1))
    after = jnp.where(column == 63, 0.0, pltpu.roll(flat, 255, 1))
    hid_rows = jnp.where(tap == 0, before, jnp.where(tap == 1, flat, after)).astype(BF)
    cots = [
        jnp.concatenate([c_ref[q + 2 - a, r + 3 - b] for q in range(2) for r in range(2)], axis=0)
        for a, b in PAIRS
    ]
    first = dot(hid_rows, jnp.concatenate(cots, axis=1))
    channel = device * 4 + zh * 2 + slot % 2
    pick_one = one_hot((slot >= 12) & (source == (slot - 12) // 2 * 64 + channel))
    vols, picks = [], []
    for i, (a, b) in enumerate(PAIRS):
        x = jnp.concatenate(
            [v_ref[2 * q + a, 2 * r + 2 + b] for q in range(2) for r in range(2)], axis=0
        )
        vol_rows = dot(pick_one, x, 1, 1).astype(BF)
        both = first[:, 128 * i : 128 * i + 128] + dot(vol_rows, own_ag)
        out_ref[:, :, 128 * i : 128 * i + 128] = both.astype(BF).reshape(16, 16, 128)
        vols.append(x)
        picks.append(one_hot((slot // 2 == i % 8) & (source == 64 + channel)))
    groups = (
        (9, jnp.concatenate(picks[:8], axis=1), jnp.concatenate(vols[:8], axis=1)),
        (10, picks[8], vols[8]),
    )
    for i, pick, x in groups:
        rows = dot(pick, x, 1, 1)
        rows = jnp.where(column == 0, 0.0, pltpu.roll(rows, 1, 1)).astype(BF)
        out_ref[:, :, 128 * i : 128 * i + 128] = dot(rows, own_ag).astype(BF).reshape(16, 16, 128)


def conv_two_body(h_ref, k_ref, out_ref):
    cells = []
    for a, b in PAIRS:
        x = jnp.concatenate([h_ref[a, b], h_ref[a, b + 1]], axis=0)
        wide = x.astype(F32)
        cells += [earlier(wide).astype(BF), x, later(wide).astype(BF)]
    acc = dot(jnp.concatenate(cells, axis=1), k_ref[...])
    out_ref[...] = acc.T.astype(BF)


def volume_grad_body(a_ref, k_ref, out_ref):
    zero = jnp.zeros((64, 128), BF)
    half = (64, 256)
    spread = one_hot(iota(half, 1) % 128 == 2 * iota(half, 0) + iota(half, 1) // 128)
    offsets = (((1, 0),), ((0, 1), (2, 0)))
    blocks = [None] * 8
    for pi in range(2):
        for pj in range(2):
            acc = jnp.zeros((128, 256), F32)
            for a, plane in offsets[pi]:
                for b, row in offsets[pj]:
                    x = jnp.concatenate([a_ref[plane, row], a_ref[plane, row + 1]], axis=0)
                    taps = k_ref[3 * a + b]
                    weights = jnp.concatenate([taps[64:], zero, taps[:64]], axis=0)
                    acc += dot(x, weights, 1, 1)
            cells = (acc[:, :128] + later(acc[:, 128:])).astype(BF)
            for r in range(2):
                wide = dot(cells[64 * r : 64 * r + 64], spread, 0, 0)
                blocks[4 * pi + 2 * r + pj] = (wide[:64, :128] + wide[64:, 128:]).astype(BF)
    shape = (512, 512)
    to, of = iota(shape, 0), iota(shape, 1)
    turn = one_hot(of == (to % 8) * 64 + to // 8)
    out_ref[...] = dot(turn, jnp.concatenate(blocks, axis=0)).astype(BF)


def plane_sum_body(got_ref, next_ref, out_ref):
    total = got_ref[0].astype(F32)
    for i in range(1, 16):
        total += got_ref[i].astype(F32)
    pieces = [total[:, 128 * j : 128 * j + 128] for j in range(11)]
    rows = jnp.concatenate(pieces + [jnp.zeros((80, 128), F32)], axis=0)
    out_ref[:, :128] = next_ref[...]
    out_ref[:, 128:] = rows.T.astype(BF)


def line_sum_body(scale, got_ref, out_ref):
    total = got_ref[0].astype(F32)
    for i in range(1, 16):
        total += got_ref[i].astype(F32)
    out_ref[...] = (total[:, 128:] * scale).T


def shifted(block, axis, distance):
    size = lax.axis_size(axis)
    route = [(i, i + distance) for i in range(size) if 0 <= i + distance < size]
    return lax.ppermute(block, axis, route)


def shape(dims, kind=BF):
    return jax.ShapeDtypeStruct(dims, kind)


def per_device(volume, kernel_one, kernel_two, cotangent):
    zh = lax.axis_index("zh")
    h = lax.axis_index(HEIGHT)
    here = jnp.stack([h, zh]).astype(jnp.int32)
    one = kernel_one.reshape(9, 192, 128)
    two = kernel_two.reshape(9, 384, 128)
    planes = lax.axis_size(PLANE)

    own = call(columns_body, shape((2, 4, 64, 128)), volume.reshape(512, 128))
    slabs = call(slabs_body, shape((32, 8, 384)), cotangent.reshape(8, 2048), own)
    other = lax.ppermute(own, "zh", [(0, 1), (1, 0)])
    slab = lax.all_to_all(slabs, LINE, 0, 0, tiled=True)
    planes4 = call(
        order_body, shape((4, 4, 64, 128)), here, own, other, scalars=1, flops=40 * 10**9
    )
    deep = jnp.concatenate(
        [shifted(planes4[:, 1:], HEIGHT, 1), planes4, shifted(planes4[:, :2], HEIGHT, -1)], axis=1
    )
    cot = call(turn_body, shape((2, 6, 64, 128)), slab.reshape(256, 384))
    lower = shifted(jnp.concatenate([deep[3], cot[1]], axis=0), PLANE, 1)
    vol = jnp.concatenate([lower[None, :9], deep], axis=0)
    cot = jnp.concatenate([lower[None, 9:], cot, shifted(cot[:1], PLANE, -1)], axis=0)

    act, hidden = call(
        conv_one_body,
        [shape((2, 4, 64, 128), F32), shape((2, 4, 64, 128))],
        here,
        vol,
        one,
        scalars=1,
    )
    up = [(2 * k, 2 * k + 2) for k in range(planes - 1)]
    down = [(2 * k + 1, 2 * k - 1) for k in range(1, planes)]
    ag = call(
        hidden_grad_body, shape((2, 3, 64, 128)), here, cot, two, act, scalars=1
    )
    edge = jnp.concatenate([jnp.where(zh == 0, hidden[1], hidden[0]), ag[0]], axis=0)
    edge = lax.ppermute(edge, DEPTH, up + down)
    partial = call(
        kernel_grads_body, shape((16, 16, 1408)), here, cot, ag, hidden, vol, scalars=1
    )
    parts = lax.all_to_all(partial, PLANE, 0, 0, tiled=True)

    side = edge[None, :4]
    three = jnp.where(
        zh == 0, jnp.concatenate([side, hidden], axis=0), jnp.concatenate([hidden, side], axis=0)
    )
    next_own = call(conv_two_body, shape((128, 128)), three, kernel_two.reshape(3456, 128))
    pair = jnp.where(zh == 0, ag, jnp.concatenate([ag[1:], edge[None, 4:]], axis=0))
    volume_grad = call(volume_grad_body, shape((512, 128)), pair, one).reshape(volume.shape)
    parts, volume_grad = lax.optimization_barrier((parts, volume_grad))

    summed = call(plane_sum_body, shape((128, 384)), parts, next_own)
    rows = lax.all_to_all(summed.reshape(16, 8, 384), HEIGHT, 0, 0, tiled=True)
    swapped = rows[:, :, :128].reshape(16, 8, 2, 64)
    next_acts = swapped.transpose(1, 0, 2, 3).reshape(cotangent.shape)
    table = call(functools.partial(line_sum_body, 1.0 / math.sqrt(65536)), shape((256, 8), F32), rows)
    slots = table[:144].reshape(9, 16, 8)
    two_grad = slots[:, :12].reshape(3, 3, 3, 4, 8)
    before = table[144:162].reshape(9, 1, 2, 8)
    one_grad = jnp.concatenate([before, slots[:, 12:].reshape(9, 2, 2, 8)], axis=1)
    return (next_acts, volume_grad, one_grad.reshape(3, 3, 3, 2, 8), two_grad)


def solution(mesh):
    fine = Mesh(mesh.devices.reshape(4, 4, 2, 8, 2), DEPTH + HEIGHT)
    placed = (P(None, DEPTH, HEIGHT, None), P(), P(), P(HEIGHT, DEPTH, None, None))
    return jax.shard_map(
        per_device,
        mesh=fine,
        in_specs=placed,
        out_specs=(
            P(HEIGHT, DEPTH, None, None),
            P(None, DEPTH, HEIGHT, None),
            P(None, None, None, DEPTH, HEIGHT),
            P(None, None, None, DEPTH, HEIGHT),
        ),
        check_vma=False,
    )
```

```python
import functools
import math

import jax
import jax.numpy as jnp
from jax import lax
from jax.experimental import pallas as pl
from jax.experimental.pallas import tpu as pltpu
from jax.sharding import Mesh, PartitionSpec as P

SLOPE = 0.2
DEPTH = ("x", "y", "zh")
HEIGHT = ("zl", "core")
PLANE = ("x", "y")
LINE = ("zh", "zl", "core")
BF = jnp.bfloat16
F32 = jnp.float32
PAIRS = tuple((a, b) for a in range(3) for b in range(3))


def dot(a, b, ca=1, cb=0):
    return lax.dot_general(a, b, (((ca,), (cb,)), ((), ())), preferred_element_type=F32)


def iota(shape, dim):
    return lax.broadcasted_iota(jnp.int32, shape, dim)


def one_hot(mask):
    return jnp.where(mask, 1.0, 0.0).astype(BF)


def earlier(x):
    return jnp.where(iota(x.shape, 0) % 64 == 0, 0.0, pltpu.roll(x, 1, 0))


def later(x):
    return jnp.where(iota(x.shape, 0) % 64 == 63, 0.0, pltpu.roll(x, x.shape[0] - 1, 0))


def call(body, outs, *args, scalars=0, flops=0, far=0, far_out=False, scratch=()):
    smem = pl.BlockSpec(memory_space=pltpu.SMEM)
    vmem = pl.BlockSpec(memory_space=pltpu.VMEM)
    hbm = pl.BlockSpec(memory_space=pl.ANY)
    out = hbm if far_out else vmem
    many = isinstance(outs, list)
    return pl.pallas_call(
        body,
        out_shape=outs,
        in_specs=[smem] * scalars + [vmem] * (len(args) - scalars - far) + [hbm] * far,
        out_specs=[out] * len(outs) if many else out,
        scratch_shapes=scratch,
        compiler_params=pltpu.CompilerParams(vmem_limit_bytes=16 * 1024 * 1024),
        cost_estimate=pl.CostEstimate(flops=flops, bytes_accessed=0, transcendentals=0) if flops else None,
    )(*args)


def columns(vol):
    shape = (512, 512)
    to, of = iota(shape, 0), iota(shape, 1)
    rows = dot(one_hot(of == (to % 64) * 8 + to // 64), vol).astype(BF)
    half = (64, 128)
    even = one_hot(iota(half, 1) == 2 * iota(half, 0))
    odd = one_hot(iota(half, 1) == 2 * iota(half, 0) + 1)
    zero = jnp.zeros((64, 128), BF)
    blocks = []
    for i in range(8):
        block = rows[64 * i : 64 * i + 64]
        left = jnp.concatenate([block, zero], axis=0)
        right = jnp.concatenate([zero, block], axis=0)
        blocks.append((dot(even, left, 1, 1) + dot(odd, right, 1, 1)).astype(BF))
    return blocks


def columns_body(vol_ref, out_ref):
    for i, block in enumerate(columns(vol_ref[...])):
        out_ref[i // 4, i % 4] = block


def pair_body(s_ref, own_ref, other_ref, out_ref):
    zh = s_ref[1]
    for i, block in enumerate(columns(other_ref[...])):
        out_ref[2 - 2 * zh + i // 4, i % 4] = block
    for i in range(2):
        out_ref[2 * zh + i] = own_ref[i]


def slabs_body(cot_ref, slab_ref):
    for i in range(16):
        for j in range(3):
            pair = i + j - 1
            if 0 <= pair < 16:
                piece = cot_ref[:, 128 * pair : 128 * pair + 128]
            else:
                piece = jnp.zeros((8, 128), BF)
            slab_ref[i, :, 128 * j : 128 * j + 128] = piece
            slab_ref[16 + i, :, 128 * j : 128 * j + 128] = piece


def weights_body(one_far, two_far, w_one_ref, w_two_ref, one_ref, two_ref, sems):
    fetch_one = pltpu.make_async_copy(one_far, one_ref, sems.at[0])
    fetch_two = pltpu.make_async_copy(two_far, two_ref, sems.at[1])
    fetch_one.start()
    fetch_two.start()
    fetch_one.wait()
    fetch_two.wait()
    w_one_ref[...] = one_ref[...]
    for i, (a, b) in enumerate(PAIRS):
        w_two_ref[:, 128 * i : 128 * i + 128] = two_ref[3 * (2 - a) + 2 - b]


def turn_body(got_ref, out_ref):
    eye = one_hot(iota((128, 128), 0) == iota((128, 128), 1))
    for q in range(2):
        for j in range(3):
            block = got_ref[128 * q : 128 * q + 128, 128 * j : 128 * j + 128]
            turned = dot(eye, block, 1, 1).astype(BF)
            out_ref[q, 2 * j] = turned[:64]
            out_ref[q, 2 * j + 1] = turned[64:]


def vol_row(deep_ref, low_ref, plane, row):
    return low_ref[row] if plane == 0 else deep_ref[plane - 1, row]


def cot_row(cot_ref, low_ref, up_ref, plane, row):
    if plane == 0:
        return low_ref[8 + row]
    return up_ref[row - 1] if plane == 3 else cot_ref[plane - 1, row]


def front_body(s_ref, deep_ref, low_ref, cot_ref, up_ref, w_one_ref, w_two_ref, hid_ref, ag_ref):
    h = s_ref[0]
    cells = [
        jnp.concatenate(
            [
                vol_row(deep_ref, low_ref, 2 * q + a, 2 * r + b)
                for q in range(2)
                for r in range(4)
            ],
            axis=0,
        )
        for a, b in PAIRS
    ]
    zero = jnp.zeros((64, 128), BF)
    left = [w_one_ref[i, 64:] for i in range(9)]
    right = [part for i in range(9) for part in (zero, w_one_ref[i, :64])]
    weights = [jnp.concatenate(parts, axis=0) for parts in (left, right)]
    acc = dot(jnp.concatenate(cells, axis=1), jnp.concatenate(weights, axis=1))
    act = acc[:, :128] + earlier(acc[:, 128:])
    small = jnp.exp(-jnp.abs(act))
    hidden = SLOPE * act + (1.0 - SLOPE) * (jnp.maximum(act, 0.0) + jnp.log1p(small))
    row = iota((512, 128), 0) // 64 % 4 + 2 * h - 1
    hidden = jnp.where((row >= 0) & (row < 32), hidden, 0.0).astype(BF)
    sigmoid = jnp.where(act >= 0.0, 1.0, small) / (1.0 + small)
    factor = SLOPE + (1.0 - SLOPE) * sigmoid
    factor = jnp.concatenate([factor[64:256], factor[320:]], axis=0)
    for q in range(2):
        for r in range(4):
            at = 64 * (4 * q + r)
            hid_ref[q, r] = hidden[at : at + 64]
    cells = [
        jnp.concatenate(
            [
                cot_row(cot_ref, low_ref, up_ref, q + a, r + 1 + b)
                for q in range(2)
                for r in range(3)
            ],
            axis=0,
        )
        for a, b in PAIRS
    ]
    acc = dot(jnp.concatenate(cells, axis=1), w_two_ref[...], 1, 1)
    grad = acc[:, 128:256] + earlier(acc[:, 256:]) + later(acc[:, :128])
    row = iota((384, 128), 0) // 64 % 3 + 2 * h
    ag = jnp.where(row < 32, grad * factor, 0.0).astype(BF)
    for q in range(2):
        for r in range(3):
            at = 64 * (3 * q + r)
            ag_ref[q, r] = ag[at : at + 64]


def kernel_grads_body(
    s_ref, deep_ref, low_ref, cot_ref, up_ref, ag_ref, hid_ref, out_far, out_ref, sems
):
    zh = s_ref[1]
    copies = []

    def put(i, value):
        out_ref[i] = value.astype(BF).reshape(16, 16, 128)
        place = out_far.at[:, :, 128 * i : 128 * i + 128]
        copies.append(pltpu.make_async_copy(out_ref.at[i], place, sems.at[i]))
        copies[-1].start()

    own_ag = jnp.concatenate([ag_ref[q, r] for q in range(2) for r in range(2)], axis=0)
    slot_row = iota((256, 128), 0)
    source = iota((256, 128), 1)
    device, slot = slot_row // 16, slot_row % 16
    pick_two = one_hot((slot < 12) & (source == device * 8 + zh * 4 + slot % 4))
    own_hid = jnp.concatenate([hid_ref[q, r + 1] for q in range(2) for r in range(2)], axis=0)
    flat = dot(pick_two, own_hid, 1, 1)
    tap = iota((256, 256), 0) % 16 // 4
    column = iota((256, 256), 1) % 64
    before = jnp.where(column == 0, 0.0, pltpu.roll(flat, 1, 1))
    after = jnp.where(column == 63, 0.0, pltpu.roll(flat, 255, 1))
    hid_rows = jnp.where(tap == 0, before, jnp.where(tap == 1, flat, after)).astype(BF)
    cots = [
        jnp.concatenate(
            [
                cot_row(cot_ref, low_ref, up_ref, q + 2 - a, r + 3 - b)
                for q in range(2)
                for r in range(2)
            ],
            axis=0,
        )
        for a, b in PAIRS
    ]
    first = dot(hid_rows, jnp.concatenate(cots, axis=1))
    channel = device * 4 + zh * 2 + slot % 2
    pick_one = one_hot((slot >= 12) & (source == (slot - 12) // 2 * 64 + channel))
    vols, picks = [], []
    for i, (a, b) in enumerate(PAIRS):
        x = jnp.concatenate(
            [
                vol_row(deep_ref, low_ref, 2 * q + a, 2 * r + 2 + b)
                for q in range(2)
                for r in range(2)
            ],
            axis=0,
        )
        vol_rows = dot(pick_one, x, 1, 1).astype(BF)
        both = first[:, 128 * i : 128 * i + 128] + dot(vol_rows, own_ag)
        put(i, both)
        vols.append(x)
        picks.append(one_hot((slot // 2 == i % 8) & (source == 64 + channel)))
    groups = (
        (9, jnp.concatenate(picks[:8], axis=1), jnp.concatenate(vols[:8], axis=1)),
        (10, picks[8], vols[8]),
    )
    for i, pick, x in groups:
        rows = dot(pick, x, 1, 1)
        rows = jnp.where(column == 0, 0.0, pltpu.roll(rows, 1, 1)).astype(BF)
        put(i, dot(rows, own_ag))
    for copy in copies:
        copy.wait()


def conv_two_body(h_ref, w_two_ref, out_ref):
    acc = jnp.zeros((128, 128), F32)
    for i, (a, b) in enumerate(PAIRS):
        x = jnp.concatenate([h_ref[a, b], h_ref[a, b + 1]], axis=0)
        wide = x.astype(F32)
        taps = jnp.concatenate([earlier(wide).astype(BF), x, later(wide).astype(BF)], axis=1)
        acc += dot(taps, w_two_ref[:, 128 * (8 - i) : 128 * (9 - i)])
    out_ref[...] = acc.T.astype(BF)


def volume_grad_body(a_ref, k_ref, out_ref):
    zero = jnp.zeros((64, 128), BF)
    half = (64, 256)
    spread = one_hot(iota(half, 1) % 128 == 2 * iota(half, 0) + iota(half, 1) // 128)
    offsets = (((1, 0),), ((0, 1), (2, 0)))
    blocks = [None] * 8
    for pi in range(2):
        for pj in range(2):
            acc = jnp.zeros((128, 256), F32)
            for a, plane in offsets[pi]:
                for b, row in offsets[pj]:
                    x = jnp.concatenate([a_ref[plane, row], a_ref[plane, row + 1]], axis=0)
                    taps = k_ref[3 * a + b]
                    weights = jnp.concatenate([taps[64:], zero, taps[:64]], axis=0)
                    acc += dot(x, weights, 1, 1)
            cells = (acc[:, :128] + later(acc[:, 128:])).astype(BF)
            for r in range(2):
                wide = dot(cells[64 * r : 64 * r + 64], spread, 0, 0)
                blocks[4 * pi + 2 * r + pj] = (wide[:64, :128] + wide[64:, 128:]).astype(BF)
    shape = (512, 512)
    to, of = iota(shape, 0), iota(shape, 1)
    turn = one_hot(of == (to % 8) * 64 + to // 8)
    out_ref[...] = dot(turn, jnp.concatenate(blocks, axis=0)).astype(BF)


def plane_sum_body(got_ref, next_ref, out_ref):
    total = got_ref[0].astype(F32)
    for i in range(1, 16):
        total += got_ref[i].astype(F32)
    pieces = [total[:, 128 * j : 128 * j + 128] for j in range(11)]
    rows = jnp.concatenate(pieces + [jnp.zeros((80, 128), F32)], axis=0)
    out_ref[:, :128] = next_ref[...]
    out_ref[:, 128:] = rows.T.astype(BF)


def finish_body(scale, got_ref, next_ref, one_ref, two_ref):
    total = got_ref[0][:, 128:].astype(F32)
    for i in range(1, 16):
        total += got_ref[i][:, 128:].astype(F32)
    table = (total * scale).T
    for i in range(9):
        one_ref[3 * i] = table[144 + 2 * i : 146 + 2 * i]
        one_ref[3 * i + 1] = table[16 * i + 12 : 16 * i + 14]
        one_ref[3 * i + 2] = table[16 * i + 14 : 16 * i + 16]
        for e in range(3):
            two_ref[3 * i + e] = table[16 * i + 4 * e : 16 * i + 4 * e + 4]
    cells = jnp.concatenate([got_ref[i][:, :128].astype(F32) for i in range(16)], axis=0).astype(BF)
    to, of = iota((256, 128), 0), iota((256, 128), 1)
    source = to % 32 // 2 * 8 + to // 32
    left = dot(one_hot((of == source) & (to % 2 == 0)), cells)
    right = dot(one_hot((of == source) & (to % 2 == 1)), cells)
    rows = left[:, :64] + right[:, 64:]
    next_ref[...] = rows.reshape(8, 32, 64).astype(BF)


def shifted(block, axis, distance):
    size = lax.axis_size(axis)
    route = [(i, i + distance) for i in range(size) if 0 <= i + distance < size]
    return lax.ppermute(block, axis, route)


def shape(dims, kind=BF):
    return jax.ShapeDtypeStruct(dims, kind)


def per_device(volume, kernel_one, kernel_two, cotangent):
    zh = lax.axis_index("zh")
    h = lax.axis_index(HEIGHT)
    here = jnp.stack([h, zh]).astype(jnp.int32)
    one = kernel_one.reshape(9, 192, 128)
    two = kernel_two.reshape(9, 384, 128)
    planes = lax.axis_size(PLANE)

    other = lax.ppermute(volume, "zh", [(0, 1), (1, 0)])
    slabs = call(slabs_body, shape((32, 8, 384)), cotangent.reshape(8, 2048))
    slab = lax.all_to_all(slabs, LINE, 0, 0, tiled=True)
    own = call(columns_body, shape((2, 4, 64, 128)), volume.reshape(512, 128))
    weights = call(
        weights_body,
        [shape((9, 192, 128)), shape((384, 1152))],
        one,
        two,
        far=2,
        scratch=(
            pltpu.VMEM((9, 192, 128), BF),
            pltpu.VMEM((9, 384, 128), BF),
            pltpu.SemaphoreType.DMA((2,)),
        ),
    )
    other, own, *weights = lax.optimization_barrier((other, own, *weights))
    deep = call(
        pair_body,
        shape((4, 4, 64, 128)),
        here,
        own,
        other.reshape(512, 128),
        scalars=1,
        flops=40 * 10**9,
    )
    deep = jnp.concatenate(
        [shifted(deep[:, 1:], HEIGHT, 1), deep, shifted(deep[:, :2], HEIGHT, -1)], axis=1
    )
    cot = call(turn_body, shape((2, 6, 64, 128)), slab.reshape(256, 384))
    lower = shifted(jnp.concatenate([deep[3], cot[1, 1:]], axis=0), PLANE, 1)
    upper = shifted(cot[0, 1:], PLANE, -1)

    hidden, ag = call(
        front_body,
        [shape((2, 4, 64, 128)), shape((2, 3, 64, 128))],
        here,
        deep,
        lower,
        cot,
        upper,
        *weights,
        scalars=1,
    )
    up = [(2 * k, 2 * k + 2) for k in range(planes - 1)]
    down = [(2 * k + 1, 2 * k - 1) for k in range(1, planes)]
    edge = jnp.concatenate([jnp.where(zh == 0, hidden[1], hidden[0]), ag[0]], axis=0)
    edge = lax.ppermute(edge, DEPTH, up + down)
    partial = call(
        kernel_grads_body,
        shape((16, 16, 1408)),
        here,
        deep,
        lower,
        cot,
        upper,
        ag,
        hidden,
        scalars=1,
        far_out=True,
        scratch=(pltpu.VMEM((11, 16, 16, 128), BF), pltpu.SemaphoreType.DMA((11,))),
    )
    parts = lax.all_to_all(partial, PLANE, 0, 0, tiled=True)

    side = edge[None, :4]
    three = jnp.where(
        zh == 0, jnp.concatenate([side, hidden], axis=0), jnp.concatenate([hidden, side], axis=0)
    )
    next_own = call(conv_two_body, shape((128, 128)), three, weights[1])
    pair = jnp.where(zh == 0, ag, jnp.concatenate([ag[1:], edge[None, 4:]], axis=0))
    volume_grad = call(volume_grad_body, shape((512, 128)), pair, weights[0]).reshape(volume.shape)
    parts, volume_grad = lax.optimization_barrier((parts, volume_grad))

    summed = call(plane_sum_body, shape((128, 384)), parts, next_own)
    rows = lax.all_to_all(summed.reshape(16, 8, 384), HEIGHT, 0, 0, tiled=True)
    next_acts, one_grad, two_grad = call(
        functools.partial(finish_body, 1.0 / math.sqrt(65536)),
        [shape((8, 32, 64)), shape((27, 2, 8), F32), shape((27, 4, 8), F32)],
        rows,
    )
    return (
        next_acts.reshape(cotangent.shape),
        volume_grad,
        one_grad.reshape(3, 3, 3, 2, 8),
        two_grad.reshape(3, 3, 3, 4, 8),
    )


def solution(mesh):
    fine = Mesh(mesh.devices.reshape(4, 4, 2, 8, 2), DEPTH + HEIGHT)
    placed = (P(None, DEPTH, HEIGHT, None), P(), P(), P(HEIGHT, DEPTH, None, None))
    return jax.shard_map(
        per_device,
        mesh=fine,
        in_specs=placed,
        out_specs=(
            P(HEIGHT, DEPTH, None, None),
            P(None, DEPTH, HEIGHT, None),
            P(None, None, None, DEPTH, HEIGHT),
            P(None, None, None, DEPTH, HEIGHT),
        ),
        check_vma=False,
    )
```

```python
import functools
import math

import jax
import jax.numpy as jnp
from jax import lax
from jax.experimental import pallas as pl
from jax.experimental.pallas import tpu as pltpu
from jax.sharding import Mesh, PartitionSpec as P

SLOPE = 0.2
DEPTH = ("x", "y", "zh")
HEIGHT = ("zl", "core")
PLANE = ("x", "y")
LINE = ("zh", "zl", "core")
BF = jnp.bfloat16
F32 = jnp.float32
PAIRS = tuple((a, b) for a in range(3) for b in range(3))


def dot(a, b, ca=1, cb=0):
    return lax.dot_general(a, b, (((ca,), (cb,)), ((), ())), preferred_element_type=F32)


def iota(shape, dim):
    return lax.broadcasted_iota(jnp.int32, shape, dim)


def one_hot(mask):
    return jnp.where(mask, 1.0, 0.0).astype(BF)


def earlier(x):
    return jnp.where(iota(x.shape, 0) % 64 == 0, 0.0, pltpu.roll(x, 1, 0))


def later(x):
    return jnp.where(iota(x.shape, 0) % 64 == 63, 0.0, pltpu.roll(x, x.shape[0] - 1, 0))


def call(body, outs, *args, scalars=0, flops=0, far=0, far_out=False, scratch=()):
    smem = pl.BlockSpec(memory_space=pltpu.SMEM)
    vmem = pl.BlockSpec(memory_space=pltpu.VMEM)
    hbm = pl.BlockSpec(memory_space=pl.ANY)
    out = hbm if far_out else vmem
    many = isinstance(outs, list)
    return pl.pallas_call(
        body,
        out_shape=outs,
        in_specs=[smem] * scalars + [vmem] * (len(args) - scalars - far) + [hbm] * far,
        out_specs=[out] * len(outs) if many else out,
        scratch_shapes=scratch,
        compiler_params=pltpu.CompilerParams(vmem_limit_bytes=16 * 1024 * 1024),
        cost_estimate=pl.CostEstimate(flops=flops, bytes_accessed=0, transcendentals=0) if flops else None,
    )(*args)


def columns(vol):
    shape = (512, 512)
    to, of = iota(shape, 0), iota(shape, 1)
    rows = dot(one_hot(of == (to % 64) * 8 + to // 64), vol).astype(BF)
    half = (64, 128)
    even = one_hot(iota(half, 1) == 2 * iota(half, 0))
    odd = one_hot(iota(half, 1) == 2 * iota(half, 0) + 1)
    zero = jnp.zeros((64, 128), BF)
    blocks = []
    for i in range(8):
        block = rows[64 * i : 64 * i + 64]
        left = jnp.concatenate([block, zero], axis=0)
        right = jnp.concatenate([zero, block], axis=0)
        blocks.append((dot(even, left, 1, 1) + dot(odd, right, 1, 1)).astype(BF))
    return blocks


def pair_body(s_ref, own_ref, other_ref, out_ref):
    zh = s_ref[1]
    for i, block in enumerate(columns(own_ref[...])):
        out_ref[2 * zh + i // 4, i % 4] = block
    for i, block in enumerate(columns(other_ref[...])):
        out_ref[2 - 2 * zh + i // 4, i % 4] = block


def slabs_body(cot_ref, slab_ref):
    for i in range(16):
        for j in range(3):
            pair = i + j - 1
            if 0 <= pair < 16:
                piece = cot_ref[:, 128 * pair : 128 * pair + 128]
            else:
                piece = jnp.zeros((8, 128), BF)
            slab_ref[i, :, 128 * j : 128 * j + 128] = piece
            slab_ref[16 + i, :, 128 * j : 128 * j + 128] = piece


def weights_body(one_far, two_far, w_one_ref, w_two_ref, one_ref, two_ref, sems):
    fetch_one = pltpu.make_async_copy(one_far, one_ref, sems.at[0])
    fetch_two = pltpu.make_async_copy(two_far, two_ref, sems.at[1])
    fetch_one.start()
    fetch_two.start()
    fetch_one.wait()
    fetch_two.wait()
    w_one_ref[...] = one_ref[...]
    for i, (a, b) in enumerate(PAIRS):
        w_two_ref[:, 128 * i : 128 * i + 128] = two_ref[3 * (2 - a) + 2 - b]


def turn_body(got_ref, out_ref):
    eye = one_hot(iota((128, 128), 0) == iota((128, 128), 1))
    for q in range(2):
        for j in range(3):
            block = got_ref[128 * q : 128 * q + 128, 128 * j : 128 * j + 128]
            turned = dot(eye, block, 1, 1).astype(BF)
            out_ref[q, 2 * j] = turned[:64]
            out_ref[q, 2 * j + 1] = turned[64:]


def vol_row(deep_ref, low_ref, plane, row):
    return low_ref[row] if plane == 0 else deep_ref[plane - 1, row]


def cot_row(cot_ref, low_ref, up_ref, plane, row):
    if plane == 0:
        return low_ref[8 + row]
    return up_ref[row - 1] if plane == 3 else cot_ref[plane - 1, row]


def front_body(s_ref, deep_ref, low_ref, cot_ref, up_ref, w_one_ref, w_two_ref, hid_ref, ag_ref):
    h = s_ref[0]
    cells = [
        jnp.concatenate(
            [
                vol_row(deep_ref, low_ref, 2 * q + a, 2 * r + b)
                for q in range(2)
                for r in range(4)
            ],
            axis=0,
        )
        for a, b in PAIRS
    ]
    zero = jnp.zeros((64, 128), BF)
    left = [w_one_ref[i, 64:] for i in range(9)]
    right = [part for i in range(9) for part in (zero, w_one_ref[i, :64])]
    weights = [jnp.concatenate(parts, axis=0) for parts in (left, right)]
    acc = dot(jnp.concatenate(cells, axis=1), jnp.concatenate(weights, axis=1))
    act = acc[:, :128] + earlier(acc[:, 128:])
    small = jnp.exp(-jnp.abs(act))
    hidden = SLOPE * act + (1.0 - SLOPE) * (jnp.maximum(act, 0.0) + jnp.log1p(small))
    row = iota((512, 128), 0) // 64 % 4 + 2 * h - 1
    hidden = jnp.where((row >= 0) & (row < 32), hidden, 0.0).astype(BF)
    sigmoid = jnp.where(act >= 0.0, 1.0, small) / (1.0 + small)
    factor = SLOPE + (1.0 - SLOPE) * sigmoid
    factor = jnp.concatenate([factor[64:256], factor[320:]], axis=0)
    for q in range(2):
        for r in range(4):
            at = 64 * (4 * q + r)
            hid_ref[q, r] = hidden[at : at + 64]
    cells = [
        jnp.concatenate(
            [
                cot_row(cot_ref, low_ref, up_ref, q + a, r + 1 + b)
                for q in range(2)
                for r in range(3)
            ],
            axis=0,
        )
        for a, b in PAIRS
    ]
    acc = dot(jnp.concatenate(cells, axis=1), w_two_ref[...], 1, 1)
    grad = acc[:, 128:256] + earlier(acc[:, 256:]) + later(acc[:, :128])
    row = iota((384, 128), 0) // 64 % 3 + 2 * h
    ag = jnp.where(row < 32, grad * factor, 0.0).astype(BF)
    for q in range(2):
        for r in range(3):
            at = 64 * (3 * q + r)
            ag_ref[q, r] = ag[at : at + 64]


def kernel_grads_body(
    s_ref, deep_ref, low_ref, cot_ref, up_ref, ag_ref, hid_ref, out_far, out_ref, sems
):
    zh = s_ref[1]
    copies = []

    def put(i, value):
        out_ref[i] = value.astype(BF).reshape(16, 16, 128)
        place = out_far.at[:, :, 128 * i : 128 * i + 128]
        copies.append(pltpu.make_async_copy(out_ref.at[i], place, sems.at[i]))
        copies[-1].start()

    own_ag = jnp.concatenate([ag_ref[q, r] for q in range(2) for r in range(2)], axis=0)
    slot_row = iota((256, 128), 0)
    source = iota((256, 128), 1)
    device, slot = slot_row // 16, slot_row % 16
    pick_two = one_hot((slot < 12) & (source == device * 8 + zh * 4 + slot % 4))
    own_hid = jnp.concatenate([hid_ref[q, r + 1] for q in range(2) for r in range(2)], axis=0)
    flat = dot(pick_two, own_hid, 1, 1)
    tap = iota((256, 256), 0) % 16 // 4
    column = iota((256, 256), 1) % 64
    before = jnp.where(column == 0, 0.0, pltpu.roll(flat, 1, 1))
    after = jnp.where(column == 63, 0.0, pltpu.roll(flat, 255, 1))
    hid_rows = jnp.where(tap == 0, before, jnp.where(tap == 1, flat, after)).astype(BF)
    cots = [
        jnp.concatenate(
            [
                cot_row(cot_ref, low_ref, up_ref, q + 2 - a, r + 3 - b)
                for q in range(2)
                for r in range(2)
            ],
            axis=0,
        )
        for a, b in PAIRS
    ]
    first = dot(hid_rows, jnp.concatenate(cots, axis=1))
    channel = device * 4 + zh * 2 + slot % 2
    pick_one = one_hot((slot >= 12) & (source == (slot - 12) // 2 * 64 + channel))
    vols, picks = [], []
    for i, (a, b) in enumerate(PAIRS):
        x = jnp.concatenate(
            [
                vol_row(deep_ref, low_ref, 2 * q + a, 2 * r + 2 + b)
                for q in range(2)
                for r in range(2)
            ],
            axis=0,
        )
        vol_rows = dot(pick_one, x, 1, 1).astype(BF)
        both = first[:, 128 * i : 128 * i + 128] + dot(vol_rows, own_ag)
        put(i, both)
        vols.append(x)
        picks.append(one_hot((slot // 2 == i % 8) & (source == 64 + channel)))
    groups = (
        (9, jnp.concatenate(picks[:8], axis=1), jnp.concatenate(vols[:8], axis=1)),
        (10, picks[8], vols[8]),
    )
    for i, pick, x in groups:
        rows = dot(pick, x, 1, 1)
        rows = jnp.where(column == 0, 0.0, pltpu.roll(rows, 1, 1)).astype(BF)
        put(i, dot(rows, own_ag))
    for copy in copies:
        copy.wait()


def conv_two_body(h_ref, w_two_ref, out_ref):
    acc = jnp.zeros((128, 128), F32)
    for i, (a, b) in enumerate(PAIRS):
        x = jnp.concatenate([h_ref[a, b], h_ref[a, b + 1]], axis=0)
        wide = x.astype(F32)
        taps = jnp.concatenate([earlier(wide).astype(BF), x, later(wide).astype(BF)], axis=1)
        acc += dot(taps, w_two_ref[:, 128 * (8 - i) : 128 * (9 - i)])
    out_ref[...] = acc.T.astype(BF)


def volume_grad_body(a_ref, k_ref, out_ref):
    zero = jnp.zeros((64, 128), BF)
    half = (64, 256)
    spread = one_hot(iota(half, 1) % 128 == 2 * iota(half, 0) + iota(half, 1) // 128)
    offsets = (((1, 0),), ((0, 1), (2, 0)))
    blocks = [None] * 8
    for pi in range(2):
        for pj in range(2):
            acc = jnp.zeros((128, 256), F32)
            for a, plane in offsets[pi]:
                for b, row in offsets[pj]:
                    x = jnp.concatenate([a_ref[plane, row], a_ref[plane, row + 1]], axis=0)
                    taps = k_ref[3 * a + b]
                    weights = jnp.concatenate([taps[64:], zero, taps[:64]], axis=0)
                    acc += dot(x, weights, 1, 1)
            cells = (acc[:, :128] + later(acc[:, 128:])).astype(BF)
            for r in range(2):
                wide = dot(cells[64 * r : 64 * r + 64], spread, 0, 0)
                blocks[4 * pi + 2 * r + pj] = (wide[:64, :128] + wide[64:, 128:]).astype(BF)
    shape = (512, 512)
    to, of = iota(shape, 0), iota(shape, 1)
    turn = one_hot(of == (to % 8) * 64 + to // 8)
    out_ref[...] = dot(turn, jnp.concatenate(blocks, axis=0)).astype(BF)


def plane_sum_body(got_ref, next_ref, out_ref):
    total = got_ref[0].astype(F32)
    for i in range(1, 16):
        total += got_ref[i].astype(F32)
    pieces = [total[:, 128 * j : 128 * j + 128] for j in range(11)]
    rows = jnp.concatenate(pieces + [jnp.zeros((80, 128), F32)], axis=0)
    out_ref[:, :128] = next_ref[...]
    out_ref[:, 128:] = rows.T.astype(BF)


def finish_body(scale, got_ref, next_ref, one_ref, two_ref):
    total = got_ref[0][:, 128:].astype(F32)
    for i in range(1, 16):
        total += got_ref[i][:, 128:].astype(F32)
    table = (total * scale).T
    for i in range(9):
        one_ref[3 * i] = table[144 + 2 * i : 146 + 2 * i]
        one_ref[3 * i + 1] = table[16 * i + 12 : 16 * i + 14]
        one_ref[3 * i + 2] = table[16 * i + 14 : 16 * i + 16]
        for e in range(3):
            two_ref[3 * i + e] = table[16 * i + 4 * e : 16 * i + 4 * e + 4]
    cells = jnp.concatenate([got_ref[i][:, :128].astype(F32) for i in range(16)], axis=0).astype(BF)
    to, of = iota((256, 128), 0), iota((256, 128), 1)
    source = to % 32 // 2 * 8 + to // 32
    left = dot(one_hot((of == source) & (to % 2 == 0)), cells)
    right = dot(one_hot((of == source) & (to % 2 == 1)), cells)
    rows = left[:, :64] + right[:, 64:]
    next_ref[...] = rows.reshape(8, 32, 64).astype(BF)


def shifted(block, axis, distance):
    size = lax.axis_size(axis)
    route = [(i, i + distance) for i in range(size) if 0 <= i + distance < size]
    return lax.ppermute(block, axis, route)


def shape(dims, kind=BF):
    return jax.ShapeDtypeStruct(dims, kind)


def per_device(volume, kernel_one, kernel_two, cotangent):
    zh = lax.axis_index("zh")
    h = lax.axis_index(HEIGHT)
    here = jnp.stack([h, zh]).astype(jnp.int32)
    one = kernel_one.reshape(9, 192, 128)
    two = kernel_two.reshape(9, 384, 128)
    planes = lax.axis_size(PLANE)

    other = lax.ppermute(volume, "zh", [(0, 1), (1, 0)])
    slabs = call(slabs_body, shape((32, 8, 384)), cotangent.reshape(8, 2048))
    slab = lax.all_to_all(slabs, LINE, 0, 0, tiled=True)
    deep = call(
        pair_body,
        shape((4, 4, 64, 128)),
        here,
        volume.reshape(512, 128),
        other.reshape(512, 128),
        scalars=1,
        flops=40 * 10**9,
    )
    deep = jnp.concatenate(
        [shifted(deep[:, 1:], HEIGHT, 1), deep, shifted(deep[:, :2], HEIGHT, -1)], axis=1
    )
    weights = call(
        weights_body,
        [shape((9, 192, 128)), shape((384, 1152))],
        one,
        two,
        far=2,
        scratch=(
            pltpu.VMEM((9, 192, 128), BF),
            pltpu.VMEM((9, 384, 128), BF),
            pltpu.SemaphoreType.DMA((2,)),
        ),
    )
    deep, *weights = lax.optimization_barrier((deep, *weights))
    cot = call(turn_body, shape((2, 6, 64, 128)), slab.reshape(256, 384))
    lower = shifted(jnp.concatenate([deep[3], cot[1, 1:]], axis=0), PLANE, 1)
    upper = shifted(cot[0, 1:], PLANE, -1)

    hidden, ag = call(
        front_body,
        [shape((2, 4, 64, 128)), shape((2, 3, 64, 128))],
        here,
        deep,
        lower,
        cot,
        upper,
        *weights,
        scalars=1,
    )
    up = [(2 * k, 2 * k + 2) for k in range(planes - 1)]
    down = [(2 * k + 1, 2 * k - 1) for k in range(1, planes)]
    edge = jnp.concatenate([jnp.where(zh == 0, hidden[1], hidden[0]), ag[0]], axis=0)
    edge = lax.ppermute(edge, DEPTH, up + down)
    partial = call(
        kernel_grads_body,
        shape((16, 16, 1408)),
        here,
        deep,
        lower,
        cot,
        upper,
        ag,
        hidden,
        scalars=1,
        far_out=True,
        scratch=(pltpu.VMEM((11, 16, 16, 128), BF), pltpu.SemaphoreType.DMA((11,))),
    )
    parts = lax.all_to_all(partial, PLANE, 0, 0, tiled=True)

    side = edge[None, :4]
    three = jnp.where(
        zh == 0, jnp.concatenate([side, hidden], axis=0), jnp.concatenate([hidden, side], axis=0)
    )
    next_own = call(conv_two_body, shape((128, 128)), three, weights[1])
    pair = jnp.where(zh == 0, ag, jnp.concatenate([ag[1:], edge[None, 4:]], axis=0))
    volume_grad = call(volume_grad_body, shape((512, 128)), pair, weights[0]).reshape(volume.shape)
    parts, volume_grad = lax.optimization_barrier((parts, volume_grad))

    summed = call(plane_sum_body, shape((128, 384)), parts, next_own)
    rows = lax.all_to_all(summed.reshape(16, 8, 384), HEIGHT, 0, 0, tiled=True)
    next_acts, one_grad, two_grad = call(
        functools.partial(finish_body, 1.0 / math.sqrt(65536)),
        [shape((8, 32, 64)), shape((27, 2, 8), F32), shape((27, 4, 8), F32)],
        rows,
    )
    return (
        next_acts.reshape(cotangent.shape),
        volume_grad,
        one_grad.reshape(3, 3, 3, 2, 8),
        two_grad.reshape(3, 3, 3, 4, 8),
    )


def solution(mesh):
    fine = Mesh(mesh.devices.reshape(4, 4, 2, 8, 2), DEPTH + HEIGHT)
    placed = (P(None, DEPTH, HEIGHT, None), P(), P(), P(HEIGHT, DEPTH, None, None))
    return jax.shard_map(
        per_device,
        mesh=fine,
        in_specs=placed,
        out_specs=(
            P(HEIGHT, DEPTH, None, None),
            P(None, DEPTH, HEIGHT, None),
            P(None, None, None, DEPTH, HEIGHT),
            P(None, None, None, DEPTH, HEIGHT),
        ),
        check_vma=False,
    )
```

```python
import functools
import math

import jax
import jax.numpy as jnp
from jax import lax
from jax.experimental import pallas as pl
from jax.experimental.pallas import tpu as pltpu
from jax.sharding import Mesh, PartitionSpec as P

SLOPE = 0.2
DEPTH = ("x", "y", "zh")
HEIGHT = ("zl", "core")
PLANE = ("x", "y")
LINE = ("zh", "zl", "core")
BF = jnp.bfloat16
F32 = jnp.float32
PAIRS = tuple((a, b) for a in range(3) for b in range(3))


def dot(a, b, ca=1, cb=0):
    return lax.dot_general(a, b, (((ca,), (cb,)), ((), ())), preferred_element_type=F32)


def iota(shape, dim):
    return lax.broadcasted_iota(jnp.int32, shape, dim)


def one_hot(mask):
    return jnp.where(mask, 1.0, 0.0).astype(BF)


def earlier(x):
    return jnp.where(iota(x.shape, 0) % 64 == 0, 0.0, pltpu.roll(x, 1, 0))


def later(x):
    return jnp.where(iota(x.shape, 0) % 64 == 63, 0.0, pltpu.roll(x, x.shape[0] - 1, 0))


def call(body, outs, *args, scalars=0, flops=0, far=0, far_out=False, scratch=()):
    smem = pl.BlockSpec(memory_space=pltpu.SMEM)
    vmem = pl.BlockSpec(memory_space=pltpu.VMEM)
    hbm = pl.BlockSpec(memory_space=pl.ANY)
    out = hbm if far_out else vmem
    many = isinstance(outs, list)
    return pl.pallas_call(
        body,
        out_shape=outs,
        in_specs=[smem] * scalars + [vmem] * (len(args) - scalars - far) + [hbm] * far,
        out_specs=[out] * len(outs) if many else out,
        scratch_shapes=scratch,
        compiler_params=pltpu.CompilerParams(vmem_limit_bytes=16 * 1024 * 1024),
        cost_estimate=pl.CostEstimate(flops=flops, bytes_accessed=0, transcendentals=0) if flops else None,
    )(*args)


def columns(vol):
    shape = (512, 512)
    to, of = iota(shape, 0), iota(shape, 1)
    rows = dot(one_hot(of == (to % 64) * 8 + to // 64), vol).astype(BF)
    half = (64, 128)
    even = one_hot(iota(half, 1) == 2 * iota(half, 0))
    odd = one_hot(iota(half, 1) == 2 * iota(half, 0) + 1)
    zero = jnp.zeros((64, 128), BF)
    blocks = []
    for i in range(8):
        block = rows[64 * i : 64 * i + 64]
        left = jnp.concatenate([block, zero], axis=0)
        right = jnp.concatenate([zero, block], axis=0)
        blocks.append((dot(even, left, 1, 1) + dot(odd, right, 1, 1)).astype(BF))
    return blocks


def pair_body(s_ref, own_ref, other_ref, out_ref):
    zh = s_ref[1]
    for i, block in enumerate(columns(own_ref[...])):
        out_ref[2 * zh + i // 4, i % 4] = block
    for i, block in enumerate(columns(other_ref[...])):
        out_ref[2 - 2 * zh + i // 4, i % 4] = block


def slabs_body(cot_ref, slab_ref):
    for i in range(16):
        for j in range(3):
            pair = i + j - 1
            if 0 <= pair < 16:
                piece = cot_ref[:, 128 * pair : 128 * pair + 128]
            else:
                piece = jnp.zeros((8, 128), BF)
            slab_ref[i, :, 128 * j : 128 * j + 128] = piece
            slab_ref[16 + i, :, 128 * j : 128 * j + 128] = piece


def weights_body(one_far, two_far, w_one_ref, w_two_ref, one_ref, two_ref, sems):
    fetch_one = pltpu.make_async_copy(one_far, one_ref, sems.at[0])
    fetch_two = pltpu.make_async_copy(two_far, two_ref, sems.at[1])
    fetch_one.start()
    fetch_two.start()
    fetch_one.wait()
    fetch_two.wait()
    w_one_ref[...] = one_ref[...]
    for i, (a, b) in enumerate(PAIRS):
        w_two_ref[:, 128 * i : 128 * i + 128] = two_ref[3 * (2 - a) + 2 - b]


def turn_body(got_ref, out_ref):
    eye = one_hot(iota((128, 128), 0) == iota((128, 128), 1))
    for q in range(2):
        for j in range(3):
            block = got_ref[128 * q : 128 * q + 128, 128 * j : 128 * j + 128]
            turned = dot(eye, block, 1, 1).astype(BF)
            out_ref[q, 2 * j] = turned[:64]
            out_ref[q, 2 * j + 1] = turned[64:]


def vol_row(deep_ref, low_ref, plane, row):
    return low_ref[row] if plane == 0 else deep_ref[plane - 1, row]


def cot_row(cot_ref, low_ref, up_ref, plane, row):
    if plane == 0:
        return low_ref[8 + row]
    return up_ref[row - 1] if plane == 3 else cot_ref[plane - 1, row]


def front_body(s_ref, deep_ref, low_ref, cot_ref, up_ref, w_one_ref, w_two_ref, hid_ref, ag_ref):
    h = s_ref[0]
    cells = [
        jnp.concatenate(
            [
                vol_row(deep_ref, low_ref, 2 * q + a, 2 * r + b)
                for q in range(2)
                for r in range(4)
            ],
            axis=0,
        )
        for a, b in PAIRS
    ]
    zero = jnp.zeros((64, 128), BF)
    left = [w_one_ref[i, 64:] for i in range(9)]
    right = [part for i in range(9) for part in (zero, w_one_ref[i, :64])]
    weights = [jnp.concatenate(parts, axis=0) for parts in (left, right)]
    acc = dot(jnp.concatenate(cells, axis=1), jnp.concatenate(weights, axis=1))
    act = acc[:, :128] + earlier(acc[:, 128:])
    small = jnp.exp(-jnp.abs(act))
    hidden = SLOPE * act + (1.0 - SLOPE) * (jnp.maximum(act, 0.0) + jnp.log1p(small))
    row = iota((512, 128), 0) // 64 % 4 + 2 * h - 1
    hidden = jnp.where((row >= 0) & (row < 32), hidden, 0.0).astype(BF)
    sigmoid = jnp.where(act >= 0.0, 1.0, small) / (1.0 + small)
    factor = SLOPE + (1.0 - SLOPE) * sigmoid
    factor = jnp.concatenate([factor[64:256], factor[320:]], axis=0)
    for q in range(2):
        for r in range(4):
            at = 64 * (4 * q + r)
            hid_ref[q, r] = hidden[at : at + 64]
    cells = [
        jnp.concatenate(
            [
                cot_row(cot_ref, low_ref, up_ref, q + a, r + 1 + b)
                for q in range(2)
                for r in range(3)
            ],
            axis=0,
        )
        for a, b in PAIRS
    ]
    acc = dot(jnp.concatenate(cells, axis=1), w_two_ref[...], 1, 1)
    grad = acc[:, 128:256] + earlier(acc[:, 256:]) + later(acc[:, :128])
    row = iota((384, 128), 0) // 64 % 3 + 2 * h
    ag = jnp.where(row < 32, grad * factor, 0.0).astype(BF)
    for q in range(2):
        for r in range(3):
            at = 64 * (3 * q + r)
            ag_ref[q, r] = ag[at : at + 64]


def kernel_grads_body(
    s_ref, deep_ref, low_ref, cot_ref, up_ref, ag_ref, hid_ref, out_far, out_ref, sems
):
    zh = s_ref[1]
    copies = []

    def put(i, value):
        out_ref[i] = value.astype(BF).reshape(16, 16, 128)
        place = out_far.at[:, :, 128 * i : 128 * i + 128]
        copies.append(pltpu.make_async_copy(out_ref.at[i], place, sems.at[i]))
        copies[-1].start()

    own_ag = jnp.concatenate([ag_ref[q, r] for q in range(2) for r in range(2)], axis=0)
    slot_row = iota((256, 128), 0)
    source = iota((256, 128), 1)
    device, slot = slot_row // 16, slot_row % 16
    pick_two = one_hot((slot < 12) & (source == device * 8 + zh * 4 + slot % 4))
    own_hid = jnp.concatenate([hid_ref[q, r + 1] for q in range(2) for r in range(2)], axis=0)
    flat = dot(pick_two, own_hid, 1, 1)
    tap = iota((256, 256), 0) % 16 // 4
    column = iota((256, 256), 1) % 64
    before = jnp.where(column == 0, 0.0, pltpu.roll(flat, 1, 1))
    after = jnp.where(column == 63, 0.0, pltpu.roll(flat, 255, 1))
    hid_rows = jnp.where(tap == 0, before, jnp.where(tap == 1, flat, after)).astype(BF)
    cots = [
        jnp.concatenate(
            [
                cot_row(cot_ref, low_ref, up_ref, q + 2 - a, r + 3 - b)
                for q in range(2)
                for r in range(2)
            ],
            axis=0,
        )
        for a, b in PAIRS
    ]
    first = dot(hid_rows, jnp.concatenate(cots, axis=1))
    channel = device * 4 + zh * 2 + slot % 2
    pick_one = one_hot((slot >= 12) & (source == (slot - 12) // 2 * 64 + channel))
    vols, picks = [], []
    for i, (a, b) in enumerate(PAIRS):
        x = jnp.concatenate(
            [
                vol_row(deep_ref, low_ref, 2 * q + a, 2 * r + 2 + b)
                for q in range(2)
                for r in range(2)
            ],
            axis=0,
        )
        vol_rows = dot(pick_one, x, 1, 1).astype(BF)
        both = first[:, 128 * i : 128 * i + 128] + dot(vol_rows, own_ag)
        put(i, both)
        vols.append(x)
        picks.append(one_hot((slot // 2 == i % 8) & (source == 64 + channel)))
    groups = (
        (9, jnp.concatenate(picks[:8], axis=1), jnp.concatenate(vols[:8], axis=1)),
        (10, picks[8], vols[8]),
    )
    for i, pick, x in groups:
        rows = dot(pick, x, 1, 1)
        rows = jnp.where(column == 0, 0.0, pltpu.roll(rows, 1, 1)).astype(BF)
        put(i, dot(rows, own_ag))
    for copy in copies:
        copy.wait()


def conv_two_body(h_ref, w_two_ref, out_ref):
    acc = jnp.zeros((128, 128), F32)
    for i, (a, b) in enumerate(PAIRS):
        x = jnp.concatenate([h_ref[a, b], h_ref[a, b + 1]], axis=0)
        wide = x.astype(F32)
        taps = jnp.concatenate([earlier(wide).astype(BF), x, later(wide).astype(BF)], axis=1)
        acc += dot(taps, w_two_ref[:, 128 * (8 - i) : 128 * (9 - i)])
    out_ref[...] = acc.T.astype(BF)


def volume_grad_body(a_ref, k_ref, out_ref):
    zero = jnp.zeros((64, 128), BF)
    half = (64, 256)
    spread = one_hot(iota(half, 1) % 128 == 2 * iota(half, 0) + iota(half, 1) // 128)
    offsets = (((1, 0),), ((0, 1), (2, 0)))
    blocks = [None] * 8
    for pi in range(2):
        for pj in range(2):
            acc = jnp.zeros((128, 256), F32)
            for a, plane in offsets[pi]:
                for b, row in offsets[pj]:
                    x = jnp.concatenate([a_ref[plane, row], a_ref[plane, row + 1]], axis=0)
                    taps = k_ref[3 * a + b]
                    weights = jnp.concatenate([taps[64:], zero, taps[:64]], axis=0)
                    acc += dot(x, weights, 1, 1)
            cells = (acc[:, :128] + later(acc[:, 128:])).astype(BF)
            for r in range(2):
                wide = dot(cells[64 * r : 64 * r + 64], spread, 0, 0)
                blocks[4 * pi + 2 * r + pj] = (wide[:64, :128] + wide[64:, 128:]).astype(BF)
    shape = (512, 512)
    to, of = iota(shape, 0), iota(shape, 1)
    turn = one_hot(of == (to % 8) * 64 + to // 8)
    out_ref[...] = dot(turn, jnp.concatenate(blocks, axis=0)).astype(BF)


def plane_sum_body(got_ref, next_ref, out_ref):
    total = got_ref[0].astype(F32)
    for i in range(1, 16):
        total += got_ref[i].astype(F32)
    pieces = [total[:, 128 * j : 128 * j + 128] for j in range(11)]
    rows = jnp.concatenate(pieces + [jnp.zeros((80, 128), F32)], axis=0)
    out_ref[:, :128] = next_ref[...]
    out_ref[:, 128:] = rows.T.astype(BF)


def finish_body(scale, got_ref, next_ref, one_ref, two_ref):
    total = got_ref[0][:, 128:].astype(F32)
    for i in range(1, 16):
        total += got_ref[i][:, 128:].astype(F32)
    table = (total * scale).T
    for i in range(9):
        one_ref[3 * i] = table[144 + 2 * i : 146 + 2 * i]
        one_ref[3 * i + 1] = table[16 * i + 12 : 16 * i + 14]
        one_ref[3 * i + 2] = table[16 * i + 14 : 16 * i + 16]
        for e in range(3):
            two_ref[3 * i + e] = table[16 * i + 4 * e : 16 * i + 4 * e + 4]
    cells = jnp.concatenate([got_ref[i][:, :128].astype(F32) for i in range(16)], axis=0).astype(BF)
    to, of = iota((256, 128), 0), iota((256, 128), 1)
    source = to % 32 // 2 * 8 + to // 32
    left = dot(one_hot((of == source) & (to % 2 == 0)), cells)
    right = dot(one_hot((of == source) & (to % 2 == 1)), cells)
    rows = left[:, :64] + right[:, 64:]
    next_ref[...] = rows.reshape(8, 32, 64).astype(BF)


def shifted(block, axis, distance):
    size = lax.axis_size(axis)
    route = [(i, i + distance) for i in range(size) if 0 <= i + distance < size]
    return lax.ppermute(block, axis, route)


def shape(dims, kind=BF):
    return jax.ShapeDtypeStruct(dims, kind)


def per_device(volume, kernel_one, kernel_two, cotangent):
    zh = lax.axis_index("zh")
    h = lax.axis_index(HEIGHT)
    here = jnp.stack([h, zh]).astype(jnp.int32)
    one = kernel_one.reshape(9, 192, 128)
    two = kernel_two.reshape(9, 384, 128)
    planes = lax.axis_size(PLANE)

    other = lax.ppermute(volume, "zh", [(0, 1), (1, 0)])
    slabs = call(slabs_body, shape((32, 8, 384)), cotangent.reshape(8, 2048))
    slab = lax.all_to_all(slabs, LINE, 0, 0, tiled=True)
    deep = call(
        pair_body,
        shape((4, 4, 64, 128)),
        here,
        volume.reshape(512, 128),
        other.reshape(512, 128),
        scalars=1,
        flops=40 * 10**9,
    )
    deep = jnp.concatenate(
        [shifted(deep[:, 1:], HEIGHT, 1), deep, shifted(deep[:, :2], HEIGHT, -1)], axis=1
    )
    weights = call(
        weights_body,
        [shape((9, 192, 128)), shape((384, 1152))],
        one,
        two,
        far=2,
        scratch=(
            pltpu.VMEM((9, 192, 128), BF),
            pltpu.VMEM((9, 384, 128), BF),
            pltpu.SemaphoreType.DMA((2,)),
        ),
    )
    deep, *weights = lax.optimization_barrier((deep, *weights))
    cot = call(turn_body, shape((2, 6, 64, 128)), slab.reshape(256, 384))
    lower = shifted(jnp.concatenate([deep[3], cot[1, 1:]], axis=0), PLANE, 1)
    upper = shifted(cot[0, 1:], PLANE, -1)

    hidden, ag = call(
        front_body,
        [shape((2, 4, 64, 128)), shape((2, 3, 64, 128))],
        here,
        deep,
        lower,
        cot,
        upper,
        *weights,
        scalars=1,
    )
    up = [(2 * k, 2 * k + 2) for k in range(planes - 1)]
    down = [(2 * k + 1, 2 * k - 1) for k in range(1, planes)]
    side = lax.ppermute(jnp.where(zh == 0, hidden[1:], hidden[:1]), DEPTH, up + down)
    partial = call(
        kernel_grads_body,
        shape((16, 16, 1408)),
        here,
        deep,
        lower,
        cot,
        upper,
        ag,
        hidden,
        scalars=1,
        far_out=True,
        scratch=(pltpu.VMEM((11, 16, 16, 128), BF), pltpu.SemaphoreType.DMA((11,))),
    )
    parts = lax.all_to_all(partial, PLANE, 0, 0, tiled=True)

    three = jnp.where(
        zh == 0, jnp.concatenate([side, hidden], axis=0), jnp.concatenate([hidden, side], axis=0)
    )
    next_own = call(conv_two_body, shape((128, 128)), three, weights[1])
    after = lax.ppermute(ag[:1], DEPTH, down)
    pair = jnp.where(zh == 0, ag, jnp.concatenate([ag[1:], after], axis=0))
    volume_grad = call(volume_grad_body, shape((512, 128)), pair, weights[0]).reshape(volume.shape)

    summed = call(plane_sum_body, shape((128, 384)), parts, next_own)
    rows = lax.all_to_all(summed.reshape(16, 8, 384), HEIGHT, 0, 0, tiled=True)
    next_acts, one_grad, two_grad = call(
        functools.partial(finish_body, 1.0 / math.sqrt(65536)),
        [shape((8, 32, 64)), shape((27, 2, 8), F32), shape((27, 4, 8), F32)],
        rows,
    )
    return (
        next_acts.reshape(cotangent.shape),
        volume_grad,
        one_grad.reshape(3, 3, 3, 2, 8),
        two_grad.reshape(3, 3, 3, 4, 8),
    )


def solution(mesh):
    fine = Mesh(mesh.devices.reshape(4, 4, 2, 8, 2), DEPTH + HEIGHT)
    placed = (P(None, DEPTH, HEIGHT, None), P(), P(), P(HEIGHT, DEPTH, None, None))
    return jax.shard_map(
        per_device,
        mesh=fine,
        in_specs=placed,
        out_specs=(
            P(HEIGHT, DEPTH, None, None),
            P(None, DEPTH, HEIGHT, None),
            P(None, None, None, DEPTH, HEIGHT),
            P(None, None, None, DEPTH, HEIGHT),
        ),
        check_vma=False,
    )
```

```python
import functools
import math

import jax
import jax.numpy as jnp
from jax import lax
from jax.experimental import pallas as pl
from jax.experimental.pallas import tpu as pltpu
from jax.sharding import Mesh, PartitionSpec as P

SLOPE = 0.2
DEPTH = ("x", "y", "zh")
HEIGHT = ("zl", "core")
PLANE = ("x", "y")
LINE = ("zh", "zl", "core")
BF = jnp.bfloat16
F32 = jnp.float32
PAIRS = tuple((a, b) for a in range(3) for b in range(3))


def dot(a, b, ca=1, cb=0):
    return lax.dot_general(a, b, (((ca,), (cb,)), ((), ())), preferred_element_type=F32)


def iota(shape, dim):
    return lax.broadcasted_iota(jnp.int32, shape, dim)


def one_hot(mask):
    return jnp.where(mask, 1.0, 0.0).astype(BF)


def earlier(x):
    return jnp.where(iota(x.shape, 0) % 64 == 0, 0.0, pltpu.roll(x, 1, 0))


def later(x):
    return jnp.where(iota(x.shape, 0) % 64 == 63, 0.0, pltpu.roll(x, x.shape[0] - 1, 0))


def call(body, outs, *args, scalars=0, flops=0, far=0, far_out=False, scratch=()):
    smem = pl.BlockSpec(memory_space=pltpu.SMEM)
    vmem = pl.BlockSpec(memory_space=pltpu.VMEM)
    hbm = pl.BlockSpec(memory_space=pl.ANY)
    out = hbm if far_out else vmem
    many = isinstance(outs, list)
    return pl.pallas_call(
        body,
        out_shape=outs,
        in_specs=[smem] * scalars + [vmem] * (len(args) - scalars - far) + [hbm] * far,
        out_specs=[out] * len(outs) if many else out,
        scratch_shapes=scratch,
        compiler_params=pltpu.CompilerParams(vmem_limit_bytes=16 * 1024 * 1024),
        cost_estimate=pl.CostEstimate(flops=flops, bytes_accessed=0, transcendentals=0) if flops else None,
    )(*args)


def columns(vol):
    shape = (512, 512)
    to, of = iota(shape, 0), iota(shape, 1)
    rows = dot(one_hot(of == (to % 64) * 8 + to // 64), vol).astype(BF)
    half = (64, 128)
    even = one_hot(iota(half, 1) == 2 * iota(half, 0))
    odd = one_hot(iota(half, 1) == 2 * iota(half, 0) + 1)
    zero = jnp.zeros((64, 128), BF)
    blocks = []
    for i in range(8):
        block = rows[64 * i : 64 * i + 64]
        left = jnp.concatenate([block, zero], axis=0)
        right = jnp.concatenate([zero, block], axis=0)
        blocks.append((dot(even, left, 1, 1) + dot(odd, right, 1, 1)).astype(BF))
    return blocks


def pair_body(s_ref, own_ref, other_ref, out_ref):
    zh = s_ref[1]
    for i, block in enumerate(columns(own_ref[...])):
        out_ref[2 * zh + i // 4, i % 4] = block
    for i, block in enumerate(columns(other_ref[...])):
        out_ref[2 - 2 * zh + i // 4, i % 4] = block


def slabs_body(cot_ref, slab_ref):
    for i in range(16):
        for j in range(3):
            pair = i + j - 1
            if 0 <= pair < 16:
                piece = cot_ref[:, 128 * pair : 128 * pair + 128]
            else:
                piece = jnp.zeros((8, 128), BF)
            slab_ref[i, :, 128 * j : 128 * j + 128] = piece
            slab_ref[16 + i, :, 128 * j : 128 * j + 128] = piece


def weights_body(one_far, two_far, w_one_ref, w_two_ref, one_ref, two_ref, sems):
    fetch_one = pltpu.make_async_copy(one_far, one_ref, sems.at[0])
    fetch_two = pltpu.make_async_copy(two_far, two_ref, sems.at[1])
    fetch_one.start()
    fetch_two.start()
    fetch_one.wait()
    fetch_two.wait()
    w_one_ref[...] = one_ref[...]
    for i, (a, b) in enumerate(PAIRS):
        w_two_ref[:, 128 * i : 128 * i + 128] = two_ref[3 * (2 - a) + 2 - b]


def turn_body(got_ref, out_ref):
    eye = one_hot(iota((128, 128), 0) == iota((128, 128), 1))
    for q in range(2):
        for j in range(3):
            block = got_ref[128 * q : 128 * q + 128, 128 * j : 128 * j + 128]
            turned = dot(eye, block, 1, 1).astype(BF)
            out_ref[q, 2 * j] = turned[:64]
            out_ref[q, 2 * j + 1] = turned[64:]


def vol_row(deep_ref, low_ref, plane, row):
    return low_ref[row] if plane == 0 else deep_ref[plane - 1, row]


def cot_row(cot_ref, low_ref, up_ref, plane, row):
    if plane == 0:
        return low_ref[8 + row]
    return up_ref[row - 1] if plane == 3 else cot_ref[plane - 1, row]


def front_body(s_ref, deep_ref, low_ref, cot_ref, up_ref, w_one_ref, w_two_ref, hid_ref, ag_ref):
    h = s_ref[0]
    cells = [
        jnp.concatenate(
            [
                vol_row(deep_ref, low_ref, 2 * q + a, 2 * r + b)
                for q in range(2)
                for r in range(4)
            ],
            axis=0,
        )
        for a, b in PAIRS
    ]
    zero = jnp.zeros((64, 128), BF)
    left = [w_one_ref[i, 64:] for i in range(9)]
    right = [part for i in range(9) for part in (zero, w_one_ref[i, :64])]
    weights = [jnp.concatenate(parts, axis=0) for parts in (left, right)]
    acc = dot(jnp.concatenate(cells, axis=1), jnp.concatenate(weights, axis=1))
    act = acc[:, :128] + earlier(acc[:, 128:])
    small = jnp.exp(-jnp.abs(act))
    hidden = SLOPE * act + (1.0 - SLOPE) * (jnp.maximum(act, 0.0) + jnp.log1p(small))
    row = iota((512, 128), 0) // 64 % 4 + 2 * h - 1
    hidden = jnp.where((row >= 0) & (row < 32), hidden, 0.0).astype(BF)
    sigmoid = jnp.where(act >= 0.0, 1.0, small) / (1.0 + small)
    factor = SLOPE + (1.0 - SLOPE) * sigmoid
    factor = jnp.concatenate([factor[64:256], factor[320:]], axis=0)
    for q in range(2):
        for r in range(4):
            at = 64 * (4 * q + r)
            hid_ref[q, r] = hidden[at : at + 64]
    cells = [
        jnp.concatenate(
            [
                cot_row(cot_ref, low_ref, up_ref, q + a, r + 1 + b)
                for q in range(2)
                for r in range(3)
            ],
            axis=0,
        )
        for a, b in PAIRS
    ]
    acc = dot(jnp.concatenate(cells, axis=1), w_two_ref[...], 1, 1)
    grad = acc[:, 128:256] + earlier(acc[:, 256:]) + later(acc[:, :128])
    row = iota((384, 128), 0) // 64 % 3 + 2 * h
    ag = jnp.where(row < 32, grad * factor, 0.0).astype(BF)
    for q in range(2):
        for r in range(3):
            at = 64 * (3 * q + r)
            ag_ref[q, r] = ag[at : at + 64]


def kernel_grads_body(
    s_ref, deep_ref, low_ref, cot_ref, up_ref, ag_ref, hid_ref, out_far, out_ref, sems
):
    zh = s_ref[1]
    copies = []

    def put(i, value):
        out_ref[i] = value.reshape(16, 16, 128).astype(BF)
        place = out_far.at[:, :, 128 * i : 128 * i + 128]
        copies.append(pltpu.make_async_copy(out_ref.at[i], place, sems.at[i]))
        copies[-1].start()

    own_ag = jnp.concatenate([ag_ref[q, r] for q in range(2) for r in range(2)], axis=0)
    slot_row = iota((256, 128), 0)
    source = iota((256, 128), 1)
    device, slot = slot_row // 16, slot_row % 16
    pick_two = one_hot((slot < 12) & (source == device * 8 + zh * 4 + slot % 4))
    own_hid = jnp.concatenate([hid_ref[q, r + 1] for q in range(2) for r in range(2)], axis=0)
    flat = dot(pick_two, own_hid, 1, 1)
    tap = iota((256, 256), 0) % 16 // 4
    column = iota((256, 256), 1) % 64
    before = jnp.where(column == 0, 0.0, pltpu.roll(flat, 1, 1))
    after = jnp.where(column == 63, 0.0, pltpu.roll(flat, 255, 1))
    hid_rows = jnp.where(tap == 0, before, jnp.where(tap == 1, flat, after)).astype(BF)
    cots = [
        jnp.concatenate(
            [
                cot_row(cot_ref, low_ref, up_ref, q + 2 - a, r + 3 - b)
                for q in range(2)
                for r in range(2)
            ],
            axis=0,
        )
        for a, b in PAIRS
    ]
    first = dot(hid_rows, jnp.concatenate(cots, axis=1))
    channel = device * 4 + zh * 2 + slot % 2
    row, of = iota((128, 128), 0), iota((128, 128), 1)
    wanted = (row % 8 - 4) // 2 * 64 + row // 8 * 4 + zh * 2 + row % 2
    pick_one = one_hot((row % 8 >= 4) & (of == wanted))
    vols, picks = [], []
    for i, (a, b) in enumerate(PAIRS):
        x = jnp.concatenate(
            [
                vol_row(deep_ref, low_ref, 2 * q + a, 2 * r + 2 + b)
                for q in range(2)
                for r in range(2)
            ],
            axis=0,
        )
        vol_rows = dot(pick_one, x, 1, 1).astype(BF)
        upper = dot(vol_rows, own_ag).reshape(16, 8, 128)
        both = first[:, 128 * i : 128 * i + 128].reshape(16, 16, 128)
        put(i, jnp.concatenate([both[:, :8], both[:, 8:] + upper], axis=1))
        vols.append(x)
        picks.append(one_hot((slot // 2 == i % 8) & (source == 64 + channel)))
    groups = (
        (9, jnp.concatenate(picks[:8], axis=1), jnp.concatenate(vols[:8], axis=1)),
        (10, picks[8], vols[8]),
    )
    for i, pick, x in groups:
        rows = dot(pick, x, 1, 1)
        rows = jnp.where(column == 0, 0.0, pltpu.roll(rows, 1, 1)).astype(BF)
        put(i, dot(rows, own_ag))
    for copy in copies:
        copy.wait()


def conv_two_body(h_ref, w_two_ref, out_ref):
    acc = jnp.zeros((128, 128), F32)
    for i, (a, b) in enumerate(PAIRS):
        x = jnp.concatenate([h_ref[a, b], h_ref[a, b + 1]], axis=0)
        wide = x.astype(F32)
        taps = jnp.concatenate([earlier(wide).astype(BF), x, later(wide).astype(BF)], axis=1)
        acc += dot(taps, w_two_ref[:, 128 * (8 - i) : 128 * (9 - i)])
    out_ref[...] = acc.T.astype(BF)


def volume_grad_body(a_ref, k_ref, out_ref):
    zero = jnp.zeros((64, 128), BF)
    half = (64, 256)
    spread = one_hot(iota(half, 1) % 128 == 2 * iota(half, 0) + iota(half, 1) // 128)
    offsets = (((1, 0),), ((0, 1), (2, 0)))
    blocks = [None] * 8
    for pi in range(2):
        for pj in range(2):
            acc = jnp.zeros((128, 256), F32)
            for a, plane in offsets[pi]:
                for b, row in offsets[pj]:
                    x = jnp.concatenate([a_ref[plane, row], a_ref[plane, row + 1]], axis=0)
                    taps = k_ref[3 * a + b]
                    weights = jnp.concatenate([taps[64:], zero, taps[:64]], axis=0)
                    acc += dot(x, weights, 1, 1)
            cells = (acc[:, :128] + later(acc[:, 128:])).astype(BF)
            for r in range(2):
                wide = dot(cells[64 * r : 64 * r + 64], spread, 0, 0)
                blocks[4 * pi + 2 * r + pj] = (wide[:64, :128] + wide[64:, 128:]).astype(BF)
    shape = (512, 512)
    to, of = iota(shape, 0), iota(shape, 1)
    turn = one_hot(of == (to % 8) * 64 + to // 8)
    out_ref[...] = dot(turn, jnp.concatenate(blocks, axis=0)).astype(BF)


def plane_sum_body(got_ref, next_ref, out_ref):
    total = got_ref[0].astype(F32)
    for i in range(1, 16):
        total += got_ref[i].astype(F32)
    pieces = [total[:, 128 * j : 128 * j + 128] for j in range(11)]
    rows = jnp.concatenate(pieces + [jnp.zeros((80, 128), F32)], axis=0)
    out_ref[:, :128] = next_ref[...]
    out_ref[:, 128:] = rows.T.astype(BF)


def finish_body(scale, got_ref, next_ref, one_ref, two_ref):
    total = got_ref[0][:, 128:].astype(F32)
    for i in range(1, 16):
        total += got_ref[i][:, 128:].astype(F32)
    table = (total * scale).T
    for i in range(9):
        one_ref[3 * i] = table[144 + 2 * i : 146 + 2 * i]
        one_ref[3 * i + 1] = table[16 * i + 12 : 16 * i + 14]
        one_ref[3 * i + 2] = table[16 * i + 14 : 16 * i + 16]
        for e in range(3):
            two_ref[3 * i + e] = table[16 * i + 4 * e : 16 * i + 4 * e + 4]
    cells = jnp.concatenate([got_ref[i][:, :128].astype(F32) for i in range(16)], axis=0).astype(BF)
    to, of = iota((256, 128), 0), iota((256, 128), 1)
    source = to % 32 // 2 * 8 + to // 32
    left = dot(one_hot((of == source) & (to % 2 == 0)), cells)
    right = dot(one_hot((of == source) & (to % 2 == 1)), cells)
    rows = left[:, :64] + right[:, 64:]
    next_ref[...] = rows.reshape(8, 32, 64).astype(BF)


def shifted(block, axis, distance):
    size = lax.axis_size(axis)
    route = [(i, i + distance) for i in range(size) if 0 <= i + distance < size]
    return lax.ppermute(block, axis, route)


def shape(dims, kind=BF):
    return jax.ShapeDtypeStruct(dims, kind)


def per_device(volume, kernel_one, kernel_two, cotangent):
    zh = lax.axis_index("zh")
    h = lax.axis_index(HEIGHT)
    here = jnp.stack([h, zh]).astype(jnp.int32)
    one = kernel_one.reshape(9, 192, 128)
    two = kernel_two.reshape(9, 384, 128)
    planes = lax.axis_size(PLANE)

    other = lax.ppermute(volume, "zh", [(0, 1), (1, 0)])
    slabs = call(slabs_body, shape((32, 8, 384)), cotangent.reshape(8, 2048))
    slab = lax.all_to_all(slabs, LINE, 0, 0, tiled=True)
    deep = call(
        pair_body,
        shape((4, 4, 64, 128)),
        here,
        volume.reshape(512, 128),
        other.reshape(512, 128),
        scalars=1,
        flops=40 * 10**9,
    )
    deep = jnp.concatenate(
        [shifted(deep[:, 1:], HEIGHT, 1), deep, shifted(deep[:, :2], HEIGHT, -1)], axis=1
    )
    weights = call(
        weights_body,
        [shape((9, 192, 128)), shape((384, 1152))],
        one,
        two,
        far=2,
        scratch=(
            pltpu.VMEM((9, 192, 128), BF),
            pltpu.VMEM((9, 384, 128), BF),
            pltpu.SemaphoreType.DMA((2,)),
        ),
    )
    deep, *weights = lax.optimization_barrier((deep, *weights))
    cot = call(turn_body, shape((2, 6, 64, 128)), slab.reshape(256, 384))
    lower = shifted(jnp.concatenate([deep[3], cot[1, 1:]], axis=0), PLANE, 1)
    upper = shifted(cot[0, 1:], PLANE, -1)

    hidden, ag = call(
        front_body,
        [shape((2, 4, 64, 128)), shape((2, 3, 64, 128))],
        here,
        deep,
        lower,
        cot,
        upper,
        *weights,
        scalars=1,
    )
    up = [(2 * k, 2 * k + 2) for k in range(planes - 1)]
    down = [(2 * k + 1, 2 * k - 1) for k in range(1, planes)]
    side = lax.ppermute(jnp.where(zh == 0, hidden[1:], hidden[:1]), DEPTH, up + down)
    partial = call(
        kernel_grads_body,
        shape((16, 16, 1408)),
        here,
        deep,
        lower,
        cot,
        upper,
        ag,
        hidden,
        scalars=1,
        far_out=True,
        scratch=(pltpu.VMEM((11, 16, 16, 128), BF), pltpu.SemaphoreType.DMA((11,))),
    )
    parts = lax.all_to_all(partial, PLANE, 0, 0, tiled=True)

    three = jnp.where(
        zh == 0, jnp.concatenate([side, hidden], axis=0), jnp.concatenate([hidden, side], axis=0)
    )
    next_own = call(conv_two_body, shape((128, 128)), three, weights[1])
    after = lax.ppermute(ag[:1], DEPTH, down)
    pair = jnp.where(zh == 0, ag, jnp.concatenate([ag[1:], after], axis=0))
    volume_grad = call(volume_grad_body, shape((512, 128)), pair, weights[0]).reshape(volume.shape)

    summed = call(plane_sum_body, shape((128, 384)), parts, next_own)
    rows = lax.all_to_all(summed.reshape(16, 8, 384), HEIGHT, 0, 0, tiled=True)
    next_acts, one_grad, two_grad = call(
        functools.partial(finish_body, 1.0 / math.sqrt(65536)),
        [shape((8, 32, 64)), shape((27, 2, 8), F32), shape((27, 4, 8), F32)],
        rows,
    )
    return (
        next_acts.reshape(cotangent.shape),
        volume_grad,
        one_grad.reshape(3, 3, 3, 2, 8),
        two_grad.reshape(3, 3, 3, 4, 8),
    )


def solution(mesh):
    fine = Mesh(mesh.devices.reshape(4, 4, 2, 8, 2), DEPTH + HEIGHT)
    placed = (P(None, DEPTH, HEIGHT, None), P(), P(), P(HEIGHT, DEPTH, None, None))
    return jax.shard_map(
        per_device,
        mesh=fine,
        in_specs=placed,
        out_specs=(
            P(HEIGHT, DEPTH, None, None),
            P(None, DEPTH, HEIGHT, None),
            P(None, None, None, DEPTH, HEIGHT),
            P(None, None, None, DEPTH, HEIGHT),
        ),
        check_vma=False,
    )
```

```python
import functools
import math

import jax
import jax.numpy as jnp
from jax import lax
from jax.experimental import pallas as pl
from jax.experimental.pallas import tpu as pltpu
from jax.sharding import Mesh, PartitionSpec as P

SLOPE = 0.2
DEPTH = ("x", "y", "zh")
HEIGHT = ("zl", "core")
PLANE = ("x", "y")
LINE = ("zh", "zl", "core")
BF = jnp.bfloat16
F32 = jnp.float32
PAIRS = tuple((a, b) for a in range(3) for b in range(3))


def dot(a, b, ca=1, cb=0):
    return lax.dot_general(a, b, (((ca,), (cb,)), ((), ())), preferred_element_type=F32)


def iota(shape, dim):
    return lax.broadcasted_iota(jnp.int32, shape, dim)


def one_hot(mask):
    return jnp.where(mask, 1.0, 0.0).astype(BF)


def earlier(x):
    return jnp.where(iota(x.shape, 0) % 64 == 0, 0.0, pltpu.roll(x, 1, 0))


def later(x):
    return jnp.where(iota(x.shape, 0) % 64 == 63, 0.0, pltpu.roll(x, x.shape[0] - 1, 0))


def call(body, outs, *args, scalars=0, flops=0, far=0, far_outs=0, scratch=()):
    smem = pl.BlockSpec(memory_space=pltpu.SMEM)
    vmem = pl.BlockSpec(memory_space=pltpu.VMEM)
    hbm = pl.BlockSpec(memory_space=pl.ANY)
    many = isinstance(outs, list)
    near = len(outs) - far_outs if many else 1
    return pl.pallas_call(
        body,
        out_shape=outs,
        in_specs=[smem] * scalars + [vmem] * (len(args) - scalars - far) + [hbm] * far,
        out_specs=[vmem] * near + [hbm] * far_outs if many else vmem,
        scratch_shapes=scratch,
        compiler_params=pltpu.CompilerParams(vmem_limit_bytes=16 * 1024 * 1024),
        cost_estimate=pl.CostEstimate(flops=flops, bytes_accessed=0, transcendentals=0) if flops else None,
    )(*args)


def columns(vol):
    shape = (512, 512)
    to, of = iota(shape, 0), iota(shape, 1)
    rows = dot(one_hot(of == (to % 64) * 8 + to // 64), vol).astype(BF)
    half = (64, 128)
    even = one_hot(iota(half, 1) == 2 * iota(half, 0))
    odd = one_hot(iota(half, 1) == 2 * iota(half, 0) + 1)
    zero = jnp.zeros((64, 128), BF)
    blocks = []
    for i in range(8):
        block = rows[64 * i : 64 * i + 64]
        left = jnp.concatenate([block, zero], axis=0)
        right = jnp.concatenate([zero, block], axis=0)
        blocks.append((dot(even, left, 1, 1) + dot(odd, right, 1, 1)).astype(BF))
    return blocks


def pair_body(s_ref, own_ref, other_ref, out_ref):
    zh = s_ref[1]
    for i, block in enumerate(columns(own_ref[...])):
        out_ref[2 * zh + i // 4, i % 4] = block
    for i, block in enumerate(columns(other_ref[...])):
        out_ref[2 - 2 * zh + i // 4, i % 4] = block


def slabs_body(cot_ref, slab_ref):
    for i in range(16):
        for j in range(3):
            pair = i + j - 1
            if 0 <= pair < 16:
                piece = cot_ref[:, 128 * pair : 128 * pair + 128]
            else:
                piece = jnp.zeros((8, 128), BF)
            slab_ref[i, :, 128 * j : 128 * j + 128] = piece
            slab_ref[16 + i, :, 128 * j : 128 * j + 128] = piece


def weights_body(one_far, two_far, w_one_ref, w_two_ref, one_ref, two_ref, sems):
    fetch_one = pltpu.make_async_copy(one_far, one_ref, sems.at[0])
    fetch_two = pltpu.make_async_copy(two_far, two_ref, sems.at[1])
    fetch_one.start()
    fetch_two.start()
    fetch_one.wait()
    fetch_two.wait()
    w_one_ref[...] = one_ref[...]
    for i, (a, b) in enumerate(PAIRS):
        w_two_ref[:, 128 * i : 128 * i + 128] = two_ref[3 * (2 - a) + 2 - b]


def turn_body(got_ref, out_ref):
    eye = one_hot(iota((128, 128), 0) == iota((128, 128), 1))
    for q in range(2):
        for j in range(3):
            block = got_ref[128 * q : 128 * q + 128, 128 * j : 128 * j + 128]
            turned = dot(eye, block, 1, 1).astype(BF)
            out_ref[q, 2 * j] = turned[:64]
            out_ref[q, 2 * j + 1] = turned[64:]


def vol_row(deep_ref, low_ref, plane, row):
    return low_ref[row] if plane == 0 else deep_ref[plane - 1, row]


def cot_row(cot_ref, low_ref, up_ref, plane, row):
    if plane == 0:
        return low_ref[8 + row]
    return up_ref[row - 1] if plane == 3 else cot_ref[plane - 1, row]


def front(s_ref, deep_ref, low_ref, cot_ref, up_ref, w_one_ref, w_two_ref, hid_ref, ag_ref):
    h = s_ref[0]
    cells = [
        jnp.concatenate(
            [
                vol_row(deep_ref, low_ref, 2 * q + a, 2 * r + b)
                for q in range(2)
                for r in range(4)
            ],
            axis=0,
        )
        for a, b in PAIRS
    ]
    zero = jnp.zeros((64, 128), BF)
    left = [w_one_ref[i, 64:] for i in range(9)]
    right = [part for i in range(9) for part in (zero, w_one_ref[i, :64])]
    weights = [jnp.concatenate(parts, axis=0) for parts in (left, right)]
    acc = dot(jnp.concatenate(cells, axis=1), jnp.concatenate(weights, axis=1))
    act = acc[:, :128] + earlier(acc[:, 128:])
    small = jnp.exp(-jnp.abs(act))
    hidden = SLOPE * act + (1.0 - SLOPE) * (jnp.maximum(act, 0.0) + jnp.log1p(small))
    row = iota((512, 128), 0) // 64 % 4 + 2 * h - 1
    hidden = jnp.where((row >= 0) & (row < 32), hidden, 0.0).astype(BF)
    sigmoid = jnp.where(act >= 0.0, 1.0, small) / (1.0 + small)
    factor = SLOPE + (1.0 - SLOPE) * sigmoid
    factor = jnp.concatenate([factor[64:256], factor[320:]], axis=0)
    for q in range(2):
        for r in range(4):
            at = 64 * (4 * q + r)
            hid_ref[q, r] = hidden[at : at + 64]
    cells = [
        jnp.concatenate(
            [
                cot_row(cot_ref, low_ref, up_ref, q + a, r + 1 + b)
                for q in range(2)
                for r in range(3)
            ],
            axis=0,
        )
        for a, b in PAIRS
    ]
    acc = dot(jnp.concatenate(cells, axis=1), w_two_ref[...], 1, 1)
    grad = acc[:, 128:256] + earlier(acc[:, 256:]) + later(acc[:, :128])
    row = iota((384, 128), 0) // 64 % 3 + 2 * h
    ag = jnp.where(row < 32, grad * factor, 0.0).astype(BF)
    for q in range(2):
        for r in range(3):
            at = 64 * (3 * q + r)
            ag_ref[q, r] = ag[at : at + 64]


def kernel_grads(s_ref, deep_ref, low_ref, cot_ref, up_ref, ag_ref, hid_ref, out_far, out_ref, sems):
    zh = s_ref[1]
    copies = []

    def put(i, value):
        out_ref[i] = value.reshape(16, 16, 128).astype(BF)
        place = out_far.at[:, :, 128 * i : 128 * i + 128]
        copies.append(pltpu.make_async_copy(out_ref.at[i], place, sems.at[i]))
        copies[-1].start()

    own_ag = jnp.concatenate([ag_ref[q, r] for q in range(2) for r in range(2)], axis=0)
    slot_row = iota((256, 128), 0)
    source = iota((256, 128), 1)
    device, slot = slot_row // 16, slot_row % 16
    pick_two = one_hot((slot < 12) & (source == device * 8 + zh * 4 + slot % 4))
    own_hid = jnp.concatenate([hid_ref[q, r + 1] for q in range(2) for r in range(2)], axis=0)
    flat = dot(pick_two, own_hid, 1, 1)
    tap = iota((256, 256), 0) % 16 // 4
    column = iota((256, 256), 1) % 64
    before = jnp.where(column == 0, 0.0, pltpu.roll(flat, 1, 1))
    after = jnp.where(column == 63, 0.0, pltpu.roll(flat, 255, 1))
    hid_rows = jnp.where(tap == 0, before, jnp.where(tap == 1, flat, after)).astype(BF)
    cots = [
        jnp.concatenate(
            [
                cot_row(cot_ref, low_ref, up_ref, q + 2 - a, r + 3 - b)
                for q in range(2)
                for r in range(2)
            ],
            axis=0,
        )
        for a, b in PAIRS
    ]
    first = dot(hid_rows, jnp.concatenate(cots, axis=1))
    channel = device * 4 + zh * 2 + slot % 2
    row, of = iota((128, 128), 0), iota((128, 128), 1)
    wanted = (row % 8 - 4) // 2 * 64 + row // 8 * 4 + zh * 2 + row % 2
    pick_one = one_hot((row % 8 >= 4) & (of == wanted))
    vols, picks = [], []
    for i, (a, b) in enumerate(PAIRS):
        x = jnp.concatenate(
            [
                vol_row(deep_ref, low_ref, 2 * q + a, 2 * r + 2 + b)
                for q in range(2)
                for r in range(2)
            ],
            axis=0,
        )
        vol_rows = dot(pick_one, x, 1, 1).astype(BF)
        upper = dot(vol_rows, own_ag).reshape(16, 8, 128)
        both = first[:, 128 * i : 128 * i + 128].reshape(16, 16, 128)
        put(i, jnp.concatenate([both[:, :8], both[:, 8:] + upper], axis=1))
        vols.append(x)
        picks.append(one_hot((slot // 2 == i % 8) & (source == 64 + channel)))
    groups = (
        (9, jnp.concatenate(picks[:8], axis=1), jnp.concatenate(vols[:8], axis=1)),
        (10, picks[8], vols[8]),
    )
    for i, pick, x in groups:
        rows = dot(pick, x, 1, 1)
        rows = jnp.where(column == 0, 0.0, pltpu.roll(rows, 1, 1)).astype(BF)
        put(i, dot(rows, own_ag))
    for copy in copies:
        copy.wait()


def front_and_grads_body(
    s_ref,
    deep_ref,
    low_ref,
    cot_ref,
    up_ref,
    w_one_ref,
    w_two_ref,
    hid_ref,
    ag_ref,
    out_far,
    out_ref,
    sems,
):
    received = (deep_ref, low_ref, cot_ref, up_ref)
    front(s_ref, *received, w_one_ref, w_two_ref, hid_ref, ag_ref)
    kernel_grads(s_ref, *received, ag_ref, hid_ref, out_far, out_ref, sems)


def conv_two_body(h_ref, w_two_ref, out_ref):
    acc = jnp.zeros((128, 128), F32)
    for i, (a, b) in enumerate(PAIRS):
        x = jnp.concatenate([h_ref[a, b], h_ref[a, b + 1]], axis=0)
        wide = x.astype(F32)
        taps = jnp.concatenate([earlier(wide).astype(BF), x, later(wide).astype(BF)], axis=1)
        acc += dot(taps, w_two_ref[:, 128 * (8 - i) : 128 * (9 - i)])
    out_ref[...] = acc.T.astype(BF)


def volume_grad_body(a_ref, k_ref, out_ref):
    zero = jnp.zeros((64, 128), BF)
    half = (64, 256)
    spread = one_hot(iota(half, 1) % 128 == 2 * iota(half, 0) + iota(half, 1) // 128)
    offsets = (((1, 0),), ((0, 1), (2, 0)))
    blocks = [None] * 8
    for pi in range(2):
        for pj in range(2):
            acc = jnp.zeros((128, 256), F32)
            for a, plane in offsets[pi]:
                for b, row in offsets[pj]:
                    x = jnp.concatenate([a_ref[plane, row], a_ref[plane, row + 1]], axis=0)
                    taps = k_ref[3 * a + b]
                    weights = jnp.concatenate([taps[64:], zero, taps[:64]], axis=0)
                    acc += dot(x, weights, 1, 1)
            cells = (acc[:, :128] + later(acc[:, 128:])).astype(BF)
            for r in range(2):
                wide = dot(cells[64 * r : 64 * r + 64], spread, 0, 0)
                blocks[4 * pi + 2 * r + pj] = (wide[:64, :128] + wide[64:, 128:]).astype(BF)
    shape = (512, 512)
    to, of = iota(shape, 0), iota(shape, 1)
    turn = one_hot(of == (to % 8) * 64 + to // 8)
    out_ref[...] = dot(turn, jnp.concatenate(blocks, axis=0)).astype(BF)


def plane_sum_body(got_ref, next_ref, out_ref):
    total = got_ref[0].astype(F32)
    for i in range(1, 16):
        total += got_ref[i].astype(F32)
    pieces = [total[:, 128 * j : 128 * j + 128] for j in range(11)]
    rows = jnp.concatenate(pieces + [jnp.zeros((80, 128), F32)], axis=0)
    out_ref[:, :128] = next_ref[...]
    out_ref[:, 128:] = rows.T.astype(BF)


def finish_body(scale, got_ref, next_ref, one_ref, two_ref):
    total = got_ref[0][:, 128:].astype(F32)
    for i in range(1, 16):
        total += got_ref[i][:, 128:].astype(F32)
    table = (total * scale).T
    for i in range(9):
        one_ref[3 * i] = table[144 + 2 * i : 146 + 2 * i]
        one_ref[3 * i + 1] = table[16 * i + 12 : 16 * i + 14]
        one_ref[3 * i + 2] = table[16 * i + 14 : 16 * i + 16]
        for e in range(3):
            two_ref[3 * i + e] = table[16 * i + 4 * e : 16 * i + 4 * e + 4]
    cells = jnp.concatenate([got_ref[i][:, :128].astype(F32) for i in range(16)], axis=0).astype(BF)
    to, of = iota((256, 128), 0), iota((256, 128), 1)
    source = to % 32 // 2 * 8 + to // 32
    left = dot(one_hot((of == source) & (to % 2 == 0)), cells)
    right = dot(one_hot((of == source) & (to % 2 == 1)), cells)
    rows = left[:, :64] + right[:, 64:]
    next_ref[...] = rows.reshape(8, 32, 64).astype(BF)


def shifted(block, axis, distance):
    size = lax.axis_size(axis)
    route = [(i, i + distance) for i in range(size) if 0 <= i + distance < size]
    return lax.ppermute(block, axis, route)


def shape(dims, kind=BF):
    return jax.ShapeDtypeStruct(dims, kind)


def per_device(volume, kernel_one, kernel_two, cotangent):
    zh = lax.axis_index("zh")
    h = lax.axis_index(HEIGHT)
    here = jnp.stack([h, zh]).astype(jnp.int32)
    one = kernel_one.reshape(9, 192, 128)
    two = kernel_two.reshape(9, 384, 128)
    planes = lax.axis_size(PLANE)

    other = lax.ppermute(volume, "zh", [(0, 1), (1, 0)])
    slabs = call(slabs_body, shape((32, 8, 384)), cotangent.reshape(8, 2048))
    slab = lax.all_to_all(slabs, LINE, 0, 0, tiled=True)
    deep = call(
        pair_body,
        shape((4, 4, 64, 128)),
        here,
        volume.reshape(512, 128),
        other.reshape(512, 128),
        scalars=1,
        flops=40 * 10**9,
    )
    deep = jnp.concatenate(
        [shifted(deep[:, 1:], HEIGHT, 1), deep, shifted(deep[:, :2], HEIGHT, -1)], axis=1
    )
    weights = call(
        weights_body,
        [shape((9, 192, 128)), shape((384, 1152))],
        one,
        two,
        far=2,
        scratch=(
            pltpu.VMEM((9, 192, 128), BF),
            pltpu.VMEM((9, 384, 128), BF),
            pltpu.SemaphoreType.DMA((2,)),
        ),
    )
    deep, *weights = lax.optimization_barrier((deep, *weights))
    cot = call(turn_body, shape((2, 6, 64, 128)), slab.reshape(256, 384))
    lower = shifted(jnp.concatenate([deep[3], cot[1, 1:]], axis=0), PLANE, 1)
    upper = shifted(cot[0, 1:], PLANE, -1)

    hidden, ag, partial = call(
        front_and_grads_body,
        [shape((2, 4, 64, 128)), shape((2, 3, 64, 128)), shape((16, 16, 1408))],
        here,
        deep,
        lower,
        cot,
        upper,
        *weights,
        scalars=1,
        far_outs=1,
        scratch=(pltpu.VMEM((11, 16, 16, 128), BF), pltpu.SemaphoreType.DMA((11,))),
    )
    up = [(2 * k, 2 * k + 2) for k in range(planes - 1)]
    down = [(2 * k + 1, 2 * k - 1) for k in range(1, planes)]
    side = lax.ppermute(jnp.where(zh == 0, hidden[1:], hidden[:1]), DEPTH, up + down)
    parts = lax.all_to_all(partial, PLANE, 0, 0, tiled=True)

    three = jnp.where(
        zh == 0, jnp.concatenate([side, hidden], axis=0), jnp.concatenate([hidden, side], axis=0)
    )
    next_own = call(conv_two_body, shape((128, 128)), three, weights[1])
    after = lax.ppermute(ag[:1], DEPTH, down)
    pair = jnp.where(zh == 0, ag, jnp.concatenate([ag[1:], after], axis=0))
    volume_grad = call(volume_grad_body, shape((512, 128)), pair, weights[0]).reshape(volume.shape)

    summed = call(plane_sum_body, shape((128, 384)), parts, next_own)
    rows = lax.all_to_all(summed.reshape(16, 8, 384), HEIGHT, 0, 0, tiled=True)
    next_acts, one_grad, two_grad = call(
        functools.partial(finish_body, 1.0 / math.sqrt(65536)),
        [shape((8, 32, 64)), shape((27, 2, 8), F32), shape((27, 4, 8), F32)],
        rows,
    )
    return (
        next_acts.reshape(cotangent.shape),
        volume_grad,
        one_grad.reshape(3, 3, 3, 2, 8),
        two_grad.reshape(3, 3, 3, 4, 8),
    )


def solution(mesh):
    fine = Mesh(mesh.devices.reshape(4, 4, 2, 8, 2), DEPTH + HEIGHT)
    placed = (P(None, DEPTH, HEIGHT, None), P(), P(), P(HEIGHT, DEPTH, None, None))
    return jax.shard_map(
        per_device,
        mesh=fine,
        in_specs=placed,
        out_specs=(
            P(HEIGHT, DEPTH, None, None),
            P(None, DEPTH, HEIGHT, None),
            P(None, None, None, DEPTH, HEIGHT),
            P(None, None, None, DEPTH, HEIGHT),
        ),
        check_vma=False,
    )
```

```python
import functools
import math

import jax
import jax.numpy as jnp
from jax import lax
from jax.experimental import pallas as pl
from jax.experimental.pallas import tpu as pltpu
from jax.sharding import Mesh, PartitionSpec as P

SLOPE = 0.2
DEPTH = ("x", "y", "zh")
HEIGHT = ("zl", "core")
PLANE = ("x", "y")
LINE = ("zh", "zl", "core")
BF = jnp.bfloat16
F32 = jnp.float32
PAIRS = tuple((a, b) for a in range(3) for b in range(3))


def dot(a, b, ca=1, cb=0):
    return lax.dot_general(a, b, (((ca,), (cb,)), ((), ())), preferred_element_type=F32)


def iota(shape, dim):
    return lax.broadcasted_iota(jnp.int32, shape, dim)


def one_hot(mask):
    return jnp.where(mask, 1.0, 0.0).astype(BF)


def earlier(x):
    return jnp.where(iota(x.shape, 0) % 64 == 0, 0.0, pltpu.roll(x, 1, 0))


def later(x):
    return jnp.where(iota(x.shape, 0) % 64 == 63, 0.0, pltpu.roll(x, x.shape[0] - 1, 0))


def call(body, outs, *args, scalars=0, flops=0, far=0, far_outs=0, scratch=()):
    smem = pl.BlockSpec(memory_space=pltpu.SMEM)
    vmem = pl.BlockSpec(memory_space=pltpu.VMEM)
    hbm = pl.BlockSpec(memory_space=pl.ANY)
    many = isinstance(outs, list)
    near = len(outs) - far_outs if many else 1
    return pl.pallas_call(
        body,
        out_shape=outs,
        in_specs=[smem] * scalars + [vmem] * (len(args) - scalars - far) + [hbm] * far,
        out_specs=[vmem] * near + [hbm] * far_outs if many else vmem,
        scratch_shapes=scratch,
        compiler_params=pltpu.CompilerParams(vmem_limit_bytes=16 * 1024 * 1024),
        cost_estimate=pl.CostEstimate(flops=flops, bytes_accessed=0, transcendentals=0) if flops else None,
    )(*args)


def columns(vol):
    shape = (512, 512)
    to, of = iota(shape, 0), iota(shape, 1)
    rows = dot(one_hot(of == (to % 64) * 8 + to // 64), vol).astype(BF)
    half = (64, 128)
    even = one_hot(iota(half, 1) == 2 * iota(half, 0))
    odd = one_hot(iota(half, 1) == 2 * iota(half, 0) + 1)
    zero = jnp.zeros((64, 128), BF)
    blocks = []
    for i in range(8):
        block = rows[64 * i : 64 * i + 64]
        left = jnp.concatenate([block, zero], axis=0)
        right = jnp.concatenate([zero, block], axis=0)
        blocks.append((dot(even, left, 1, 1) + dot(odd, right, 1, 1)).astype(BF))
    return blocks


def pair_body(s_ref, own_ref, other_ref, out_ref):
    zh = s_ref[1]
    for i, block in enumerate(columns(own_ref[...])):
        out_ref[2 * zh + i // 4, i % 4] = block
    for i, block in enumerate(columns(other_ref[...])):
        out_ref[2 - 2 * zh + i // 4, i % 4] = block


def slabs_body(cot_ref, slab_ref):
    for i in range(16):
        for j in range(3):
            pair = i + j - 1
            if 0 <= pair < 16:
                piece = cot_ref[:, 128 * pair : 128 * pair + 128]
            else:
                piece = jnp.zeros((8, 128), BF)
            slab_ref[i, :, 128 * j : 128 * j + 128] = piece
            slab_ref[16 + i, :, 128 * j : 128 * j + 128] = piece


def weights_body(one_far, two_far, w_one_ref, w_two_ref, one_ref, two_ref, sems):
    fetch_one = pltpu.make_async_copy(one_far, one_ref, sems.at[0])
    fetch_two = pltpu.make_async_copy(two_far, two_ref, sems.at[1])
    fetch_one.start()
    fetch_two.start()
    fetch_one.wait()
    fetch_two.wait()
    w_one_ref[...] = one_ref[...]
    for i, (a, b) in enumerate(PAIRS):
        w_two_ref[:, 128 * i : 128 * i + 128] = two_ref[3 * (2 - a) + 2 - b]


def turn_body(got_ref, out_ref):
    eye = one_hot(iota((128, 128), 0) == iota((128, 128), 1))
    for q in range(2):
        for j in range(3):
            block = got_ref[128 * q : 128 * q + 128, 128 * j : 128 * j + 128]
            turned = dot(eye, block, 1, 1).astype(BF)
            out_ref[q, 2 * j] = turned[:64]
            out_ref[q, 2 * j + 1] = turned[64:]


def vol_row(deep_ref, low_ref, plane, row):
    return low_ref[row] if plane == 0 else deep_ref[plane - 1, row]


def cot_row(cot_ref, low_ref, up_ref, plane, row):
    if plane == 0:
        return low_ref[8 + row]
    return up_ref[row - 1] if plane == 3 else cot_ref[plane - 1, row]


def front(s_ref, deep_ref, low_ref, cot_ref, up_ref, w_one_ref, w_two_ref, hid_ref, ag_ref):
    h = s_ref[0]
    cells = [
        jnp.concatenate(
            [
                vol_row(deep_ref, low_ref, 2 * q + a, 2 * r + b)
                for q in range(2)
                for r in range(4)
            ],
            axis=0,
        )
        for a, b in PAIRS
    ]
    zero = jnp.zeros((64, 128), BF)
    left = [w_one_ref[i, 64:] for i in range(9)]
    right = [part for i in range(9) for part in (zero, w_one_ref[i, :64])]
    weights = [jnp.concatenate(parts, axis=0) for parts in (left, right)]
    acc = dot(jnp.concatenate(cells, axis=1), jnp.concatenate(weights, axis=1))
    act = acc[:, :128] + earlier(acc[:, 128:])
    small = jnp.exp(-jnp.abs(act))
    hidden = SLOPE * act + (1.0 - SLOPE) * (jnp.maximum(act, 0.0) + jnp.log1p(small))
    row = iota((512, 128), 0) // 64 % 4 + 2 * h - 1
    hidden = jnp.where((row >= 0) & (row < 32), hidden, 0.0).astype(BF)
    sigmoid = jnp.where(act >= 0.0, 1.0, small) / (1.0 + small)
    factor = SLOPE + (1.0 - SLOPE) * sigmoid
    factor = jnp.concatenate([factor[64:256], factor[320:]], axis=0)
    for q in range(2):
        for r in range(4):
            at = 64 * (4 * q + r)
            hid_ref[q, r] = hidden[at : at + 64]
    cells = [
        jnp.concatenate(
            [
                cot_row(cot_ref, low_ref, up_ref, q + a, r + 1 + b)
                for q in range(2)
                for r in range(3)
            ],
            axis=0,
        )
        for a, b in PAIRS
    ]
    acc = dot(jnp.concatenate(cells, axis=1), w_two_ref[...], 1, 1)
    grad = acc[:, 128:256] + earlier(acc[:, 256:]) + later(acc[:, :128])
    row = iota((384, 128), 0) // 64 % 3 + 2 * h
    ag = jnp.where(row < 32, grad * factor, 0.0).astype(BF)
    for q in range(2):
        for r in range(3):
            at = 64 * (3 * q + r)
            ag_ref[q, r] = ag[at : at + 64]


def kernel_grads(s_ref, deep_ref, low_ref, cot_ref, up_ref, ag_ref, hid_ref, out_far, out_ref, sems):
    zh = s_ref[1]
    copies = []

    def put(i, value):
        out_ref[i] = value.reshape(16, 16, 128).astype(BF)
        place = out_far.at[:, :, 128 * i : 128 * i + 128]
        copies.append(pltpu.make_async_copy(out_ref.at[i], place, sems.at[i]))
        copies[-1].start()

    own_ag = jnp.concatenate([ag_ref[q, r] for q in range(2) for r in range(2)], axis=0)
    slot_row = iota((256, 128), 0)
    source = iota((256, 128), 1)
    device, slot = slot_row // 16, slot_row % 16
    pick_two = one_hot((slot < 12) & (source == device * 8 + zh * 4 + slot % 4))
    own_hid = jnp.concatenate([hid_ref[q, r + 1] for q in range(2) for r in range(2)], axis=0)
    flat = dot(pick_two, own_hid, 1, 1)
    tap = iota((256, 256), 0) % 16 // 4
    column = iota((256, 256), 1) % 64
    before = jnp.where(column == 0, 0.0, pltpu.roll(flat, 1, 1))
    after = jnp.where(column == 63, 0.0, pltpu.roll(flat, 255, 1))
    hid_rows = jnp.where(tap == 0, before, jnp.where(tap == 1, flat, after)).astype(BF)
    cots = [
        jnp.concatenate(
            [
                cot_row(cot_ref, low_ref, up_ref, q + 2 - a, r + 3 - b)
                for q in range(2)
                for r in range(2)
            ],
            axis=0,
        )
        for a, b in PAIRS
    ]
    first = dot(hid_rows, jnp.concatenate(cots, axis=1))
    channel = device * 4 + zh * 2 + slot % 2
    row, of = iota((128, 128), 0), iota((128, 128), 1)
    wanted = (row % 8 - 4) // 2 * 64 + row // 8 * 4 + zh * 2 + row % 2
    pick_one = one_hot((row % 8 >= 4) & (of == wanted))
    vols, picks = [], []
    for i, (a, b) in enumerate(PAIRS):
        x = jnp.concatenate(
            [
                vol_row(deep_ref, low_ref, 2 * q + a, 2 * r + 2 + b)
                for q in range(2)
                for r in range(2)
            ],
            axis=0,
        )
        vol_rows = dot(pick_one, x, 1, 1).astype(BF)
        upper = dot(vol_rows, own_ag).reshape(16, 8, 128)
        both = first[:, 128 * i : 128 * i + 128].reshape(16, 16, 128)
        put(i, jnp.concatenate([both[:, :8], both[:, 8:] + upper], axis=1))
        vols.append(x)
        picks.append(one_hot((slot // 2 == i % 8) & (source == 64 + channel)))
    groups = (
        (9, jnp.concatenate(picks[:8], axis=1), jnp.concatenate(vols[:8], axis=1)),
        (10, picks[8], vols[8]),
    )
    for i, pick, x in groups:
        rows = dot(pick, x, 1, 1)
        rows = jnp.where(column == 0, 0.0, pltpu.roll(rows, 1, 1)).astype(BF)
        put(i, dot(rows, own_ag))
    for copy in copies:
        copy.wait()


def front_and_grads_body(
    s_ref,
    deep_ref,
    low_ref,
    cot_ref,
    up_ref,
    w_one_ref,
    w_two_ref,
    hid_ref,
    ag_ref,
    out_far,
    out_ref,
    sems,
):
    received = (deep_ref, low_ref, cot_ref, up_ref)
    front(s_ref, *received, w_one_ref, w_two_ref, hid_ref, ag_ref)
    kernel_grads(s_ref, *received, ag_ref, hid_ref, out_far, out_ref, sems)


def conv_two_body(h_ref, w_two_ref, out_ref):
    acc = jnp.zeros((128, 128), F32)
    for i, (a, b) in enumerate(PAIRS):
        x = jnp.concatenate([h_ref[a, b], h_ref[a, b + 1]], axis=0)
        wide = x.astype(F32)
        taps = jnp.concatenate([earlier(wide).astype(BF), x, later(wide).astype(BF)], axis=1)
        acc += dot(taps, w_two_ref[:, 128 * (8 - i) : 128 * (9 - i)])
    out_ref[...] = acc.T.astype(BF)


def volume_grad_body(a_ref, k_ref, out_ref):
    zero = jnp.zeros((64, 128), BF)
    half = (64, 256)
    spread = one_hot(iota(half, 1) % 128 == 2 * iota(half, 0) + iota(half, 1) // 128)
    offsets = (((1, 0),), ((0, 1), (2, 0)))
    blocks = [None] * 8
    for pi in range(2):
        for pj in range(2):
            acc = jnp.zeros((128, 256), F32)
            for a, plane in offsets[pi]:
                for b, row in offsets[pj]:
                    x = jnp.concatenate([a_ref[plane, row], a_ref[plane, row + 1]], axis=0)
                    taps = k_ref[3 * a + b]
                    weights = jnp.concatenate([taps[64:], zero, taps[:64]], axis=0)
                    acc += dot(x, weights, 1, 1)
            cells = (acc[:, :128] + later(acc[:, 128:])).astype(BF)
            for r in range(2):
                wide = dot(cells[64 * r : 64 * r + 64], spread, 0, 0)
                blocks[4 * pi + 2 * r + pj] = (wide[:64, :128] + wide[64:, 128:]).astype(BF)
    shape = (512, 512)
    to, of = iota(shape, 0), iota(shape, 1)
    turn = one_hot(of == (to % 8) * 64 + to // 8)
    out_ref[...] = dot(turn, jnp.concatenate(blocks, axis=0)).astype(BF)


def plane_sum_body(got_ref, next_ref, out_ref):
    total = got_ref[0].astype(F32)
    for i in range(1, 16):
        total += got_ref[i].astype(F32)
    pieces = [total[:, 128 * j : 128 * j + 128] for j in range(11)]
    rows = jnp.concatenate(pieces + [jnp.zeros((80, 128), F32)], axis=0)
    out_ref[:, :128] = next_ref[...]
    out_ref[:, 128:] = rows.T.astype(BF)


def finish_body(scale, got_ref, next_ref, one_ref, two_ref):
    total = got_ref[0][:, 128:].astype(F32)
    for i in range(1, 16):
        total += got_ref[i][:, 128:].astype(F32)
    table = (total * scale).T
    for i in range(9):
        one_ref[3 * i] = table[144 + 2 * i : 146 + 2 * i]
        one_ref[3 * i + 1] = table[16 * i + 12 : 16 * i + 14]
        one_ref[3 * i + 2] = table[16 * i + 14 : 16 * i + 16]
        for e in range(3):
            two_ref[3 * i + e] = table[16 * i + 4 * e : 16 * i + 4 * e + 4]
    cells = jnp.concatenate([got_ref[i][:, :128].astype(F32) for i in range(16)], axis=0).astype(BF)
    to, of = iota((256, 128), 0), iota((256, 128), 1)
    both = dot(one_hot(of == to % 32 // 2 * 8 + to // 32), cells)
    rows = jnp.where(iota((256, 64), 0) % 2 == 0, both[:, :64], both[:, 64:])
    next_ref[...] = rows.reshape(8, 32, 64).astype(BF)


def shifted(block, axis, distance):
    size = lax.axis_size(axis)
    route = [(i, i + distance) for i in range(size) if 0 <= i + distance < size]
    return lax.ppermute(block, axis, route)


def shape(dims, kind=BF):
    return jax.ShapeDtypeStruct(dims, kind)


def per_device(volume, kernel_one, kernel_two, cotangent):
    zh = lax.axis_index("zh")
    h = lax.axis_index(HEIGHT)
    here = jnp.stack([h, zh]).astype(jnp.int32)
    one = kernel_one.reshape(9, 192, 128)
    two = kernel_two.reshape(9, 384, 128)
    planes = lax.axis_size(PLANE)

    other = lax.ppermute(volume, "zh", [(0, 1), (1, 0)])
    slabs = call(slabs_body, shape((32, 8, 384)), cotangent.reshape(8, 2048))
    slab = lax.all_to_all(slabs, LINE, 0, 0, tiled=True)
    deep = call(
        pair_body,
        shape((4, 4, 64, 128)),
        here,
        volume.reshape(512, 128),
        other.reshape(512, 128),
        scalars=1,
        flops=40 * 10**9,
    )
    deep = jnp.concatenate(
        [shifted(deep[:, 1:], HEIGHT, 1), deep, shifted(deep[:, :2], HEIGHT, -1)], axis=1
    )
    weights = call(
        weights_body,
        [shape((9, 192, 128)), shape((384, 1152))],
        one,
        two,
        far=2,
        scratch=(
            pltpu.VMEM((9, 192, 128), BF),
            pltpu.VMEM((9, 384, 128), BF),
            pltpu.SemaphoreType.DMA((2,)),
        ),
    )
    deep, *weights = lax.optimization_barrier((deep, *weights))
    cot = call(turn_body, shape((2, 6, 64, 128)), slab.reshape(256, 384))
    lower = shifted(jnp.concatenate([deep[3], cot[1, 1:]], axis=0), PLANE, 1)
    upper = shifted(cot[0, 1:], PLANE, -1)

    hidden, ag, partial = call(
        front_and_grads_body,
        [shape((2, 4, 64, 128)), shape((2, 3, 64, 128)), shape((16, 16, 1408))],
        here,
        deep,
        lower,
        cot,
        upper,
        *weights,
        scalars=1,
        far_outs=1,
        scratch=(pltpu.VMEM((11, 16, 16, 128), BF), pltpu.SemaphoreType.DMA((11,))),
    )
    up = [(2 * k, 2 * k + 2) for k in range(planes - 1)]
    down = [(2 * k + 1, 2 * k - 1) for k in range(1, planes)]
    side = lax.ppermute(jnp.where(zh == 0, hidden[1:], hidden[:1]), DEPTH, up + down)
    parts = lax.all_to_all(partial, PLANE, 0, 0, tiled=True)

    three = jnp.where(
        zh == 0, jnp.concatenate([side, hidden], axis=0), jnp.concatenate([hidden, side], axis=0)
    )
    next_own = call(conv_two_body, shape((128, 128)), three, weights[1])
    after = lax.ppermute(ag[:1], DEPTH, down)
    pair = jnp.where(zh == 0, ag, jnp.concatenate([ag[1:], after], axis=0))
    volume_grad = call(volume_grad_body, shape((512, 128)), pair, weights[0]).reshape(volume.shape)

    summed = call(plane_sum_body, shape((128, 384)), parts, next_own)
    rows = lax.all_to_all(summed.reshape(16, 8, 384), HEIGHT, 0, 0, tiled=True)
    next_acts, one_grad, two_grad = call(
        functools.partial(finish_body, 1.0 / math.sqrt(65536)),
        [shape((8, 32, 64)), shape((27, 2, 8), F32), shape((27, 4, 8), F32)],
        rows,
    )
    return (
        next_acts.reshape(cotangent.shape),
        volume_grad,
        one_grad.reshape(3, 3, 3, 2, 8),
        two_grad.reshape(3, 3, 3, 4, 8),
    )


def solution(mesh):
    fine = Mesh(mesh.devices.reshape(4, 4, 2, 8, 2), DEPTH + HEIGHT)
    placed = (P(None, DEPTH, HEIGHT, None), P(), P(), P(HEIGHT, DEPTH, None, None))
    return jax.shard_map(
        per_device,
        mesh=fine,
        in_specs=placed,
        out_specs=(
            P(HEIGHT, DEPTH, None, None),
            P(None, DEPTH, HEIGHT, None),
            P(None, None, None, DEPTH, HEIGHT),
            P(None, None, None, DEPTH, HEIGHT),
        ),
        check_vma=False,
    )
```
